512 devices in a mesh: gx: 16 (over x, y), gy: 32 (over z, core).
Axes of the slice: x: 4, y: 4, z: 16, core: 2. Of those that a mesh axis runs over, the one named last changes fastest.
Arguments:
- features: bfloat16 [1703936, 512], P(('gx', 'gy')), may hold values from -16 to 16
- sketch: bfloat16 [512, 64], replicated, may hold values from -6 to 6
Outputs:
- basis: float32 [512, 64], replicated
- codes: bfloat16 [1703936, 64], P(('gx', 'gy'))
- left_factor: float32 [1703936, 64], P(('gx', 'gy'))
The draws below stay inside these ranges and needn't reach their ends.
All inputs are finite; a program needn't handle non-finite values.
Results may differ from the reference program's by a relative error of at most 0.0065.
Values sent between devices are 32-bit elements; how exact they have to be, the bound alone decides.
No kernel may reach another device: no remote copies, remote signals or barrier semaphores. Data moves between devices by JAX's collectives and lax.ppermute only.
A program may use at most 64 MiB of HBM per device.

```python
import math
import jax
import jax.numpy as jnp
from jax import lax

D = 512
RANK = 64
ROWS_DEV = 3328
TOTAL = 1703936


def draw_features(key, part):
    key = jax.random.fold_in(key, 11)
    keys = jax.random.split(key, 8)
    blocks = TOTAL // ROWS_DEV
    base = jax.random.normal(keys[0], (TOTAL, D), jnp.float32)
    row_scale = jnp.exp(jax.random.uniform(keys[1], (TOTAL, 1), jnp.float32, -1.15, 1.15))
    col_scale = jnp.exp(jax.random.uniform(keys[2], (1, D), jnp.float32, -1.15, 1.15))
    position = jnp.arange(TOTAL, dtype=jnp.float32).reshape(TOTAL, 1) / TOTAL
    lift = jax.random.normal(keys[5], (blocks, ROWS_DEV, 1), jnp.float32)
    strength = jnp.exp(jax.random.uniform(keys[6], (blocks, 1, 1), jnp.float32, -0.5, 0.5))
    direction = jax.random.normal(keys[7], (blocks, 1, D), jnp.float32) * strength
    planted = (lift * direction).reshape(TOTAL, D)
    values = (base * row_scale * col_scale + 1.2 * planted) * (1.0 + 0.8 * position)
    return jnp.clip(values, -16.0, 16.0).astype(jnp.bfloat16)


def bell_draw(own_key, shape, spread, limit, kind=jnp.bfloat16):
    array = spread * jax.random.normal(own_key, shape, jnp.float32)
    return jnp.clip(array, min=-limit, max=limit).astype(kind)


def setup_inputs(seed: int = 0) -> dict:
    seeds = jax.random.split(jax.random.key(seed), 3)
    features = draw_features(jax.random.fold_in(seeds[2], 71), 0)
    sketch = bell_draw(seeds[1], (D, RANK), 1.0, 6.0)
    return dict(features=features, sketch=sketch)


def left_product(features, tall):
    upper = tall.astype(jnp.bfloat16)
    lower = (tall - upper.astype(jnp.float32)).astype(jnp.bfloat16)
    dims = (((0,), (0,)), ((), ()))
    return lax.dot_general(features.astype(jnp.float32), upper.astype(jnp.float32), dims, preferred_element_type=jnp.float32) + lax.dot_general(features.astype(jnp.float32), lower.astype(jnp.float32), dims, preferred_element_type=jnp.float32)

def single_pass(matrix):
    gram = jnp.dot(matrix.T, matrix, precision=lax.Precision.HIGHEST)
    factor = jnp.linalg.cholesky(gram)
    return lax.linalg.triangular_solve(factor, matrix, left_side=False, lower=True, transpose_a=True)

def orthonormal(matrix):
    for sweep in range(2):
        matrix = single_pass(matrix)
    return matrix

def reference(features, sketch):
    first = jnp.dot(features.astype(jnp.float32), sketch.astype(jnp.float32), preferred_element_type=jnp.float32)
    wide = left_product(features, first)
    estimate = orthonormal(wide).astype(jnp.bfloat16)
    second = jnp.dot(features.astype(jnp.float32), estimate.astype(jnp.float32), preferred_element_type=jnp.float32)
    tall = single_pass(second)
    left_factor = tall * math.sqrt(features.shape[0])
    projected = left_product(features, tall)
    basis = orthonormal(projected)
    codes = jnp.dot(features.astype(jnp.float32), basis.astype(jnp.bfloat16).astype(jnp.float32), preferred_element_type=jnp.float32).astype(jnp.bfloat16)
    return (basis, codes, left_factor)
```

```python
import math

import jax
import jax.numpy as jnp
from jax import lax
from jax.sharding import Mesh, PartitionSpec as P

BLOCK = 128
HIGHEST = lax.Precision.HIGHEST


def solve_right(factor, matrix):
    return lax.linalg.triangular_solve(
        factor, matrix, left_side=False, lower=True, transpose_a=True
    )


def sweep(matrix):
    gram = jnp.dot(matrix.T, matrix, precision=HIGHEST)
    return solve_right(jnp.linalg.cholesky(gram), matrix)


def orthonormal(matrix):
    return sweep(sweep(matrix))


def exchange(parts, axes):
    return lax.all_to_all(parts, axes, split_axis=0, concat_axis=0, tiled=True)


def pack(gram):
    n = gram.shape[0] // BLOCK
    cut = lambda i, j: gram[i * BLOCK : (i + 1) * BLOCK, j * BLOCK : (j + 1) * BLOCK]
    return jnp.concatenate([cut(i, j) for i in range(n) for j in range(i, n)], axis=0)


def unpack(packed, n):
    blocks = {}
    at = 0
    for i in range(n):
        for j in range(i, n):
            blocks[i, j] = packed[at : at + BLOCK]
            at += BLOCK
    rows = []
    for i in range(n):
        row = [blocks[i, j] if j >= i else blocks[j, i].T for j in range(n)]
        rows.append(jnp.concatenate(row, axis=1))
    return jnp.concatenate(rows, axis=0)


def sum_everywhere(packed):
    plane = lax.axis_size(("gx", "c"))
    rows, width = packed.shape
    share = jnp.sum(exchange(packed.reshape(plane, rows // plane, width), ("gx", "c")), axis=0)
    line = lax.axis_size("z")
    share = jnp.sum(exchange(jnp.broadcast_to(share, (line, *share.shape)), "z"), axis=0)
    whole = exchange(jnp.broadcast_to(share, (plane, *share.shape)), ("gx", "c"))
    return whole.reshape(rows, width)


def on_device(features, sketch):
    width = features.shape[1]
    scale = math.sqrt(features.shape[0] * lax.axis_size(("gx", "z", "c")))
    local = lax.dot_general(
        features, features, (((0,), (0,)), ((), ())), preferred_element_type=jnp.float32
    )
    gram = unpack(sum_everywhere(pack(local)), width // BLOCK)
    wide = jnp.dot(gram, sketch.astype(jnp.float32), precision=HIGHEST)
    estimate = orthonormal(wide).astype(jnp.bfloat16)
    near = estimate.astype(jnp.float32)
    image = jnp.dot(gram, near, precision=HIGHEST)
    factor = jnp.linalg.cholesky(jnp.dot(near.T, image, precision=HIGHEST))
    basis = orthonormal(solve_right(factor, image))
    second = jnp.dot(features, estimate, preferred_element_type=jnp.float32)
    left_factor = solve_right(factor, second) * scale
    codes = jnp.dot(
        features, basis.astype(jnp.bfloat16), preferred_element_type=jnp.float32
    ).astype(jnp.bfloat16)
    return (basis, codes, left_factor)


def solution(mesh):
    rows, columns = mesh.devices.shape
    mesh = Mesh(mesh.devices.reshape(rows, columns // 2, 2), ("gx", "z", "c"))
    split = P(("gx", "z", "c"), None)
    return jax.shard_map(
        on_device,
        mesh=mesh,
        in_specs=(split, P()),
        out_specs=(P(), split, split),
        check_vma=False,
    )
```

```python
import functools
import math

import jax
import jax.numpy as jnp
from jax import lax
from jax.experimental import pallas as pl
from jax.experimental.pallas import tpu as pltpu
from jax.sharding import Mesh, PartitionSpec as P

BLOCK = 128
HIGHEST = lax.Precision.HIGHEST
F32 = jnp.float32
BF16 = jnp.bfloat16
NT = (((1,), (1,)), ((), ()))
NN = (((1,), (0,)), ((), ()))


def dot(a, b, dims=NN, precision=None):
    return lax.dot_general(a, b, dims, precision=precision, preferred_element_type=F32)


def split3(x):
    high = x.astype(BF16)
    rest = x - high.astype(F32)
    middle = rest.astype(BF16)
    low = (rest - middle.astype(F32)).astype(BF16)
    return high, middle, low


def gram_beside_identity(rows):
    rank = rows.shape[0]
    both = jnp.concatenate([jnp.zeros_like(rows), rows], axis=0)
    gram = dot(rows, both, NT, HIGHEST)
    lane = lax.broadcasted_iota(jnp.int32, (rank, 2 * rank), 1)
    row = lax.broadcasted_iota(jnp.int32, (rank, 2 * rank), 0)
    return gram + (lane == row).astype(F32)


def eliminate(table, out):
    rank, width = table.shape
    rest = table
    for p in range(0, rank, 8):
        high = rank - p
        columns = [
            jnp.broadcast_to(rest[:, rank + p + j : rank + p + j + 1], (high, width))
            for j in range(8)
        ]
        for j in range(8):
            column = columns[j]
            pivot = column[j : j + 1, :]
            root = lax.rsqrt(pivot)
            inverse = 1.0 / pivot
            row = rest[j : j + 1, :]
            out[p + j : p + j + 1, :] = row * root
            scaled = row * inverse
            for i in range(j + 1, 8):
                columns[i] = columns[i] - column * (columns[i][j : j + 1, :] * inverse)
            rest = rest - column * scaled
        rest = rest[8:, :]


def sweep(rows, table):
    rank = rows.shape[0]
    eliminate(gram_beside_identity(rows), table)
    return dot(table[:, :rank], rows, NN, HIGHEST)


def factor_kernel(scale, packed, sketch, weights, basis, parts, table):
    rank, width = sketch.shape
    n = width // BLOCK
    at = 0
    for i in range(n):
        for j in range(i, n):
            block = packed[at : at + BLOCK, :]
            at += BLOCK
            for k, part in enumerate(split3(block)):
                parts[k, i * BLOCK : (i + 1) * BLOCK, j * BLOCK : (j + 1) * BLOCK] = part
            if j > i:
                for k, part in enumerate(split3(block.T)):
                    parts[k, j * BLOCK : (j + 1) * BLOCK, i * BLOCK : (i + 1) * BLOCK] = part

    def times_gram(rows):
        return (dot(rows, parts[2]) + dot(rows, parts[1])) + dot(rows, parts[0])

    wide = times_gram(sketch[...])
    estimate = sweep(sweep(wide, table), table).astype(BF16)
    near = estimate.astype(F32)
    image = times_gram(estimate)
    both = jnp.concatenate([jnp.zeros_like(near), near], axis=0)
    gram = dot(image, both, NT, HIGHEST)
    lane = lax.broadcasted_iota(jnp.int32, (rank, 2 * rank), 1)
    row = lax.broadcasted_iota(jnp.int32, (rank, 2 * rank), 0)
    eliminate(gram + (lane == row).astype(F32), table)
    inverse = table[:, :rank]
    for k, part in enumerate(split3(dot(inverse, near, NN, HIGHEST) * scale)):
        weights[k * rank : (k + 1) * rank, :] = part
    projected = dot(inverse, image, NN, HIGHEST)
    base = sweep(sweep(projected, table), table)
    basis[...] = base
    weights[3 * rank : 4 * rank, :] = base.astype(BF16)


def factor(packed, sketch_rows, scale):
    rank, width = sketch_rows.shape
    return pl.pallas_call(
        functools.partial(factor_kernel, scale),
        out_shape=(
            jax.ShapeDtypeStruct((4 * rank, width), BF16),
            jax.ShapeDtypeStruct((rank, width), F32),
        ),
        in_specs=[pl.BlockSpec(memory_space=pltpu.VMEM)] * 2,
        out_specs=(pl.BlockSpec(memory_space=pltpu.VMEM),) * 2,
        scratch_shapes=[
            pltpu.VMEM((3, width, width), BF16),
            pltpu.VMEM((rank, 2 * rank), F32),
        ],
        compiler_params=pltpu.CompilerParams(vmem_limit_bytes=32 * 1024 * 1024),
        name="factor",
    )(packed, sketch_rows)


def apply_kernel(features, weights, left, codes):
    rank = left.shape[0]
    out = dot(weights[...], features[...], NT)
    left[...] = (out[2 * rank : 3 * rank] + out[rank : 2 * rank]) + out[:rank]
    codes[...] = out[3 * rank :].astype(BF16)


def apply(features, weights, step):
    rows, width = features.shape
    rank = weights.shape[0] // 4
    return pl.pallas_call(
        apply_kernel,
        grid=(rows // step,),
        out_shape=(
            jax.ShapeDtypeStruct((rank, rows), F32),
            jax.ShapeDtypeStruct((rank, rows), BF16),
        ),
        in_specs=[
            pl.BlockSpec((step, width), lambda i: (i, 0)),
            pl.BlockSpec((4 * rank, width), lambda i: (0, 0)),
        ],
        out_specs=(
            pl.BlockSpec((rank, step), lambda i: (0, i)),
            pl.BlockSpec((rank, step), lambda i: (0, i)),
        ),
        compiler_params=pltpu.CompilerParams(vmem_limit_bytes=32 * 1024 * 1024),
        name="apply",
    )(features, weights)


def gram_kernel(features, packed):
    width = features.shape[1]
    n = width // BLOCK

    @pl.when(pl.program_id(0) == 0)
    def _():
        packed[...] = jnp.zeros_like(packed)

    f = features[...]
    dims = (((0,), (0,)), ((), ()))
    half = width // 2
    top = dot(f[:, :half], f, dims)
    bottom = dot(f[:, half:], f[:, half:], dims)
    at = 0
    for i in range(n):
        for j in range(i, n):
            if i < n // 2:
                src = top[i * BLOCK : (i + 1) * BLOCK, j * BLOCK : (j + 1) * BLOCK]
            else:
                a, b = i - n // 2, j - n // 2
                src = bottom[a * BLOCK : (a + 1) * BLOCK, b * BLOCK : (b + 1) * BLOCK]
            packed[at : at + BLOCK, :] += src
            at += BLOCK


def local_gram(features, step):
    rows, width = features.shape
    n = width // BLOCK
    return pl.pallas_call(
        gram_kernel,
        grid=(rows // step,),
        out_shape=jax.ShapeDtypeStruct((n * (n + 1) // 2 * BLOCK, BLOCK), F32),
        in_specs=[pl.BlockSpec((step, width), lambda i: (i, 0))],
        out_specs=pl.BlockSpec((n * (n + 1) // 2 * BLOCK, BLOCK), lambda i: (0, 0)),
        compiler_params=pltpu.CompilerParams(vmem_limit_bytes=32 * 1024 * 1024),
        name="gram",
    )(features)


def exchange(parts, axes):
    return lax.all_to_all(parts, axes, split_axis=0, concat_axis=0, tiled=True)


def sum_everywhere(packed):
    plane = lax.axis_size(("gx", "c"))
    rows, width = packed.shape
    share = jnp.sum(exchange(packed.reshape(plane, rows // plane, width), ("gx", "c")), axis=0)
    line = lax.axis_size("z")
    share = jnp.sum(exchange(jnp.broadcast_to(share, (line, *share.shape)), "z"), axis=0)
    whole = exchange(jnp.broadcast_to(share, (plane, *share.shape)), ("gx", "c"))
    return whole.reshape(rows, width)


def on_device(features, sketch):
    scale = math.sqrt(features.shape[0] * lax.axis_size(("gx", "z", "c")))
    step = features.shape[0] // 2
    packed = sum_everywhere(local_gram(features, step))
    weights, basis = factor(packed, sketch.T, scale)
    left, codes = apply(features, weights, step)
    return (basis.T, codes.T, left.T)


def solution(mesh):
    rows, columns = mesh.devices.shape
    mesh = Mesh(mesh.devices.reshape(rows, columns // 2, 2), ("gx", "z", "c"))
    split = P(("gx", "z", "c"), None)
    return jax.shard_map(
        on_device,
        mesh=mesh,
        in_specs=(split, P()),
        out_specs=(P(), split, split),
        check_vma=False,
    )
```

```python
import functools
import math

import jax
import jax.numpy as jnp
from jax import lax
from jax.experimental import pallas as pl
from jax.experimental.pallas import tpu as pltpu
from jax.sharding import Mesh, PartitionSpec as P

BLOCK = 128
ROOM = 24 * 1024 * 1024
HIGHEST = lax.Precision.HIGHEST
F32 = jnp.float32
BF16 = jnp.bfloat16
NT = (((1,), (1,)), ((), ()))
NN = (((1,), (0,)), ((), ()))
TN = (((0,), (0,)), ((), ()))


def dot(a, b, dims=NN, precision=None):
    return lax.dot_general(a, b, dims, precision=precision, preferred_element_type=F32)


def split3(x):
    high = x.astype(BF16)
    rest = x - high.astype(F32)
    middle = rest.astype(BF16)
    low = (rest - middle.astype(F32)).astype(BF16)
    return high, middle, low


def upper_blocks(n):
    return [(i, j) for i in range(n) for j in range(i, n)]


def cuts(rows, weights):
    units = rows // BLOCK
    total = sum(weights)
    edges = [0]
    for k in range(len(weights)):
        edges.append(round(units * sum(weights[: k + 1]) / total) * BLOCK)
    return list(zip(edges[:-1], edges[1:]))


def gram_kernel(plan, core_of, features, keep, send, held, arrived):
    width = features.shape[1]
    n = width // BLOCK
    half = width // 2
    copies = []
    for k, (start, stop) in enumerate(plan):
        rows = pl.ds(start, stop - start)
        copies.append(pltpu.make_async_copy(features.at[rows], held.at[rows], arrived.at[k]))
    for copy in copies[:2]:
        copy.start()
    core = core_of()
    top = bottom = None
    for k, (start, stop) in enumerate(plan):
        copies[k].wait()
        if k + 2 < len(copies):
            copies[k + 2].start()
        f = held[start:stop, :]
        a = dot(f[:, :half], f, TN)
        b = dot(f[:, half:], f[:, half:], TN)
        top = a if top is None else top + a
        bottom = b if bottom is None else bottom + b
    pieces = []
    for i, j in upper_blocks(n):
        if i < n // 2:
            src, a, b = top, i, j
        else:
            src, a, b = bottom, i - n // 2, j - n // 2
        pieces.append(src[a * BLOCK : (a + 1) * BLOCK, b * BLOCK : (b + 1) * BLOCK])
    count = len(pieces) // 2
    for k in range(count):
        rows = slice(k * BLOCK, (k + 1) * BLOCK)
        keep[rows, :] = jnp.where(core == 0, pieces[k], pieces[count + k])
        send[rows, :] = jnp.where(core == 0, pieces[count + k], pieces[k])


def local_gram(features, core_of, weights=(1, 1, 1)):
    rows, width = features.shape
    n = width // BLOCK
    half = jax.ShapeDtypeStruct((n * (n + 1) // 4 * BLOCK, BLOCK), F32)
    plan = cuts(rows, weights)
    return pl.pallas_call(
        functools.partial(gram_kernel, plan, core_of),
        out_shape=(half, half),
        in_specs=[pl.BlockSpec(memory_space=pl.ANY)],
        out_specs=(pl.BlockSpec(memory_space=pltpu.VMEM),) * 2,
        scratch_shapes=[
            pltpu.VMEM((rows, width), BF16),
            pltpu.SemaphoreType.DMA((len(plan),)),
        ],
        compiler_params=pltpu.CompilerParams(vmem_limit_bytes=ROOM),
        cost_estimate=pl.CostEstimate(
            flops=2 * rows * width * width, bytes_accessed=2 * rows * width, transcendentals=0
        ),
        name="gram",
    )(pltpu.with_memory_space_constraint(features, pltpu.HBM))


def beside_identity(gram, rank):
    lane = lax.broadcasted_iota(jnp.int32, (rank, 2 * rank), 1)
    row = lax.broadcasted_iota(jnp.int32, (rank, 2 * rank), 0)
    return gram + (lane == row).astype(F32)


def gram_of(a, b):
    both = jnp.concatenate([jnp.zeros_like(b), b], axis=0)
    return beside_identity(dot(a, both, NT, HIGHEST), a.shape[0])


def eliminate(tables, outs):
    rank, width = tables[0].shape
    rests = list(tables)
    for p in range(0, rank, 8):
        high = rank - p
        panels = [
            [
                jnp.broadcast_to(rest[:, rank + p + j : rank + p + j + 1], (high, width))
                for j in range(8)
            ]
            for rest in rests
        ]
        for j in range(8):
            for t, out in enumerate(outs):
                columns, rest = panels[t], rests[t]
                column = columns[j]
                pivot = column[j : j + 1, :]
                inverse = 1.0 / pivot
                row = rest[j : j + 1, :]
                out[p + j : p + j + 1, :] = row * lax.rsqrt(pivot)
                for i in range(j + 1, 8):
                    columns[i] = columns[i] - column * (columns[i][j : j + 1, :] * inverse)
                rests[t] = rest - column * (row * inverse)
        rests = [rest[8:, :] for rest in rests]


def nearly_identity(rows):
    rank = rows.shape[0]
    lane = lax.broadcasted_iota(jnp.int32, (rank, rank), 1)
    row = lax.broadcasted_iota(jnp.int32, (rank, rank), 0)
    eye = (lane == row).astype(F32)
    half = jnp.where(lane < row, 1.0, 0.0) + 0.5 * eye
    off = dot(rows, rows, NT, HIGHEST) - eye
    first = off * half
    square = dot(first, first, NN, HIGHEST)
    outer = dot(first, first, NT, HIGHEST) * half
    return jnp.sum(off * off), eye + ((square + outer) - first)


def finish_kernel(
    scale, plan, core_of, mine, other, sketch, features, basis, left, codes,
    parts, table, image_table, hold, weights, held, left_held, codes_held, arrived, gone,
):
    rank, width = sketch.shape
    n = width // BLOCK
    fetches = []
    for k, (start, stop) in enumerate(plan):
        rows = pl.ds(start, stop - start)
        copy = pltpu.make_async_copy(features.at[rows], held.at[rows], arrived.at[k])
        copy.start()
        fetches.append(copy)
    core = core_of()
    blocks = upper_blocks(n)
    count = len(blocks) // 2
    for k, (i, j) in enumerate(blocks):
        rows = slice(k % count * BLOCK, (k % count + 1) * BLOCK)
        block = jnp.where(core == k // count, mine[rows, :], other[rows, :])
        for q, part in enumerate(split3(block)):
            parts[q, i * BLOCK : (i + 1) * BLOCK, j * BLOCK : (j + 1) * BLOCK] = part
        if j > i:
            for q, part in enumerate(split3(block.T)):
                parts[q, j * BLOCK : (j + 1) * BLOCK, i * BLOCK : (i + 1) * BLOCK] = part

    def times_gram(rows):
        return (dot(rows, parts[2]) + dot(rows, parts[1])) + dot(rows, parts[0])

    def sweep(rows):
        eliminate([gram_of(rows, rows)], [table])
        return dot(table[:, :rank], rows, NN, HIGHEST)

    wide = sweep(times_gram(sketch[...]))
    distance, inverse = nearly_identity(wide)
    hold[...] = dot(inverse, wide, NN, HIGHEST)

    @pl.when(jnp.logical_not(distance <= 1e-5))
    def _():
        hold[...] = sweep(wide)

    estimate = hold[...].astype(BF16)
    near = estimate.astype(F32)
    image = times_gram(estimate)
    eliminate([gram_of(image, near), gram_of(image, image)], [table, image_table])
    factor = table[:, :rank]
    for k, part in enumerate(split3(dot(factor, near, NN, HIGHEST) * scale)):
        weights[k * rank : (k + 1) * rank, :] = part
    swept = dot(image_table[:, :rank], image, NN, HIGHEST)
    distance, inverse = nearly_identity(swept)
    hold[...] = dot(inverse, swept, NN, HIGHEST)

    @pl.when(jnp.logical_not(distance <= 1e-5))
    def _():
        hold[...] = sweep(sweep(dot(factor, image, NN, HIGHEST)))

    basis[...] = hold[...]
    weights[3 * rank : 4 * rank, :] = hold[...].astype(BF16)

    sends = []
    for k, (start, stop) in enumerate(plan):
        fetches[k].wait()
        columns = slice(start, stop)
        out = dot(weights[...], held[start:stop, :], NT)
        left_held[:, columns] = (out[2 * rank : 3 * rank] + out[rank : 2 * rank]) + out[:rank]
        codes_held[:, columns] = out[3 * rank :].astype(BF16)
        span = pl.ds(start, stop - start)
        for q, (source, target) in enumerate(((left_held, left), (codes_held, codes))):
            copy = pltpu.make_async_copy(source.at[:, span], target.at[:, span], gone.at[q, k])
            copy.start()
            sends.append(copy)
    for copy in sends:
        copy.wait()


def finish(mine, other, sketch_rows, features, scale, core_of, weights=(1,)):
    rank, width = sketch_rows.shape
    rows = features.shape[0]
    plan = cuts(rows, weights)
    vmem = pl.BlockSpec(memory_space=pltpu.VMEM)
    hbm = pl.BlockSpec(memory_space=pl.ANY)
    return pl.pallas_call(
        functools.partial(finish_kernel, scale, plan, core_of),
        out_shape=(
            jax.ShapeDtypeStruct((rank, width), F32),
            jax.ShapeDtypeStruct((rank, rows), F32),
            jax.ShapeDtypeStruct((rank, rows), BF16),
        ),
        in_specs=[vmem, vmem, vmem, hbm],
        out_specs=(vmem, hbm, hbm),
        scratch_shapes=[
            pltpu.VMEM((3, width, width), BF16),
            pltpu.VMEM((rank, 2 * rank), F32),
            pltpu.VMEM((rank, 2 * rank), F32),
            pltpu.VMEM((rank, width), F32),
            pltpu.VMEM((4 * rank, width), BF16),
            pltpu.VMEM((rows, width), BF16),
            pltpu.VMEM((rank, rows), F32),
            pltpu.VMEM((rank, rows), BF16),
            pltpu.SemaphoreType.DMA((len(plan),)),
            pltpu.SemaphoreType.DMA((2, len(plan))),
        ],
        compiler_params=pltpu.CompilerParams(vmem_limit_bytes=ROOM),
        name="finish",
    )(mine, other, sketch_rows, pltpu.with_memory_space_constraint(features, pltpu.HBM))


def exchange(parts, axes):
    return lax.all_to_all(parts, axes, split_axis=0, concat_axis=0, tiled=True)


def swap(x):
    return lax.ppermute(x, "c", [(0, 1), (1, 0)])


def sum_everywhere(keep, send):
    chips, line = lax.axis_size("gx"), lax.axis_size("z")
    half = keep + swap(send)
    rows, width = half.shape
    share = jnp.sum(exchange(half.reshape(chips, rows // chips, width), "gx"), axis=0)
    share = jnp.sum(exchange(jnp.broadcast_to(share, (line, *share.shape)), "z"), axis=0)
    mine = exchange(jnp.broadcast_to(share, (chips, *share.shape)), "gx").reshape(rows, width)
    return mine, swap(mine)


def core_index():
    return lax.axis_index("c")


def on_device(features, sketch):
    scale = math.sqrt(features.shape[0] * lax.axis_size(("gx", "z", "c")))
    mine, other = sum_everywhere(*local_gram(features, core_index))
    basis, left, codes = finish(mine, other, sketch.T, features, scale, core_index)
    return (basis.T, codes.T, left.T)


def solution(mesh):
    rows, columns = mesh.devices.shape
    mesh = Mesh(mesh.devices.reshape(rows, columns // 2, 2), ("gx", "z", "c"))
    split = P(("gx", "z", "c"), None)
    return jax.shard_map(
        on_device,
        mesh=mesh,
        in_specs=(split, P()),
        out_specs=(P(), split, split),
        check_vma=False,
    )
```

```python
import functools
import math

import jax
import jax.numpy as jnp
from jax import lax
from jax.experimental import pallas as pl
from jax.experimental.pallas import tpu as pltpu
from jax.sharding import Mesh, PartitionSpec as P

BLOCK = 128
ROOM = 24 * 1024 * 1024
HIGHEST = lax.Precision.HIGHEST
F32 = jnp.float32
BF16 = jnp.bfloat16
NT = (((1,), (1,)), ((), ()))
NN = (((1,), (0,)), ((), ()))
TN = (((0,), (0,)), ((), ()))


def dot(a, b, dims=NN, precision=None):
    return lax.dot_general(a, b, dims, precision=precision, preferred_element_type=F32)


def split3(x):
    high = x.astype(BF16)
    rest = x - high.astype(F32)
    middle = rest.astype(BF16)
    low = (rest - middle.astype(F32)).astype(BF16)
    return high, middle, low


def layout(n):
    pairs = [(i, j) for i in range(n) for j in range(i + 1, n)]
    count = len(pairs) // 2
    return (pairs[:count], (0, 1)), (pairs[count:], (2, 3))


def cuts(rows, weights):
    units = rows // BLOCK
    total = sum(weights)
    edges = [0]
    for k in range(len(weights)):
        edges.append(round(units * sum(weights[: k + 1]) / total) * BLOCK)
    return list(zip(edges[:-1], edges[1:]))


def gram_kernel(plan, core_of, features, keep, send, held, arrived):
    width = features.shape[1]
    n = width // BLOCK
    half = width // 2
    copies = []
    for k, (start, stop) in enumerate(plan):
        rows = pl.ds(start, stop - start)
        copies.append(pltpu.make_async_copy(features.at[rows], held.at[rows], arrived.at[k]))
    for copy in copies[:2]:
        copy.start()
    core = core_of()
    top = bottom = None
    for k, (start, stop) in enumerate(plan):
        copies[k].wait()
        if k + 2 < len(copies):
            copies[k + 2].start()
        f = held[start:stop, :]
        a = dot(f[:, :half], f, TN)
        b = dot(f[:, half:], f[:, half:], TN)
        top = a if top is None else top + a
        bottom = b if bottom is None else bottom + b
    def block(i, j):
        if i >= n // 2:
            src, i, j = bottom, i - n // 2, j - n // 2
        else:
            src = top
        return src[i * BLOCK : (i + 1) * BLOCK, j * BLOCK : (j + 1) * BLOCK]

    halves = []
    for pairs, (a, b) in layout(n):
        low = lax.broadcasted_iota(jnp.int32, (BLOCK // 2, BLOCK), 1) < BLOCK // 2
        first, second = block(a, a), block(b, b)
        corner = pltpu.roll(first[BLOCK // 2 :], BLOCK // 2, 1)
        corners = jnp.where(low, corner, second[BLOCK // 2 :])
        halves.append(
            [block(*pair) for pair in pairs]
            + [first[: BLOCK // 2], second[: BLOCK // 2], corners]
        )
    at = 0
    for zero, one in zip(*halves):
        rows = slice(at, at + zero.shape[0])
        keep[rows, :] = jnp.where(core == 0, zero, one)
        send[rows, :] = jnp.where(core == 0, one, zero)
        at += zero.shape[0]


def local_gram(features, core_of, weights=(1, 1)):
    rows, width = features.shape
    n = width // BLOCK
    half = jax.ShapeDtypeStruct((n * (2 * n + 1) * BLOCK // 8, BLOCK), F32)
    plan = cuts(rows, weights)
    return pl.pallas_call(
        functools.partial(gram_kernel, plan, core_of),
        out_shape=(half, half),
        in_specs=[pl.BlockSpec(memory_space=pl.ANY)],
        out_specs=(pl.BlockSpec(memory_space=pltpu.VMEM),) * 2,
        scratch_shapes=[
            pltpu.VMEM((rows, width), BF16),
            pltpu.SemaphoreType.DMA((len(plan),)),
        ],
        compiler_params=pltpu.CompilerParams(vmem_limit_bytes=ROOM),
        cost_estimate=pl.CostEstimate(
            flops=2 * rows * width * width, bytes_accessed=2 * rows * width, transcendentals=0
        ),
        name="gram",
    )(pltpu.with_memory_space_constraint(features, pltpu.HBM))


def beside_identity(gram, rank):
    lane = lax.broadcasted_iota(jnp.int32, (rank, 2 * rank), 1)
    row = lax.broadcasted_iota(jnp.int32, (rank, 2 * rank), 0)
    return gram + (lane == row).astype(F32)


def gram_of(a, b):
    both = jnp.concatenate([jnp.zeros_like(b), b], axis=0)
    return beside_identity(dot(a, both, NT, HIGHEST), a.shape[0])


def eliminate(tables, outs):
    rank, width = tables[0].shape
    rests = list(tables)
    for p in range(0, rank, 8):
        high = rank - p
        panels = [
            [
                jnp.broadcast_to(rest[:, rank + p + j : rank + p + j + 1], (high, width))
                for j in range(8)
            ]
            for rest in rests
        ]
        for j in range(8):
            for t, out in enumerate(outs):
                columns, rest = panels[t], rests[t]
                column = columns[j]
                pivot = column[j : j + 1, :]
                inverse = 1.0 / pivot
                row = rest[j : j + 1, :]
                out[p + j : p + j + 1, :] = row * lax.rsqrt(pivot)
                for i in range(j + 1, 8):
                    columns[i] = columns[i] - column * (columns[i][j : j + 1, :] * inverse)
                rests[t] = rest - column * (row * inverse)
        rests = [rest[8:, :] for rest in rests]


def nearly_identity(rows):
    rank = rows.shape[0]
    lane = lax.broadcasted_iota(jnp.int32, (rank, rank), 1)
    row = lax.broadcasted_iota(jnp.int32, (rank, rank), 0)
    eye = (lane == row).astype(F32)
    half = jnp.where(lane < row, 1.0, 0.0) + 0.5 * eye
    off = dot(rows, rows, NT, HIGHEST) - eye
    first = off * half
    square = dot(first, first, NN, HIGHEST)
    outer = dot(first, first, NT, HIGHEST) * half
    return jnp.sum(off * off), eye + ((square + outer) - first)


def finish_kernel(
    scale, plan, core_of, mine, other, sketch, features, basis, left, codes,
    parts, table, image_table, hold, weights, held, left_held, codes_held, arrived, gone,
):
    rank, width = sketch.shape
    n = width // BLOCK
    fetches = []
    for k, (start, stop) in enumerate(plan):
        rows = pl.ds(start, stop - start)
        copy = pltpu.make_async_copy(features.at[rows], held.at[rows], arrived.at[k])
        copy.start()
        fetches.append(copy)
    core = core_of()

    def store(i, j, block):
        for q, part in enumerate(split3(block)):
            parts[q, i * BLOCK : (i + 1) * BLOCK, j * BLOCK : (j + 1) * BLOCK] = part

    for half, (pairs, diagonal) in enumerate(layout(n)):

        def rows_at(start, size):
            rows = slice(start, start + size)
            return jnp.where(core == half, mine[rows, :], other[rows, :])

        for k, (i, j) in enumerate(pairs):
            block = rows_at(k * BLOCK, BLOCK)
            store(i, j, block)
            store(j, i, block.T)
        at = len(pairs) * BLOCK
        corners = rows_at(at + BLOCK, BLOCK // 2)
        for k, i in enumerate(diagonal):
            corner = corners if k else pltpu.roll(corners, BLOCK // 2, 1)
            block = jnp.concatenate([rows_at(at + k * BLOCK // 2, BLOCK // 2), corner], axis=0)
            lane = lax.broadcasted_iota(jnp.int32, (BLOCK, BLOCK), 1)
            row = lax.broadcasted_iota(jnp.int32, (BLOCK, BLOCK), 0)
            store(i, i, jnp.where((row >= BLOCK // 2) & (lane < BLOCK // 2), block.T, block))

    def times_gram(rows):
        return (dot(rows, parts[2]) + dot(rows, parts[1])) + dot(rows, parts[0])

    def sweep(rows):
        eliminate([gram_of(rows, rows)], [table])
        return dot(table[:, :rank], rows, NN, HIGHEST)

    wide = sweep(times_gram(sketch[...]))
    distance, inverse = nearly_identity(wide)
    hold[...] = dot(inverse, wide, NN, HIGHEST)

    @pl.when(jnp.logical_not(distance <= 1e-5))
    def _():
        hold[...] = sweep(wide)

    estimate = hold[...].astype(BF16)
    near = estimate.astype(F32)
    image = times_gram(estimate)
    eliminate([gram_of(image, near), gram_of(image, image)], [table, image_table])
    factor = table[:, :rank]
    for k, part in enumerate(split3(dot(factor, near, NN, HIGHEST) * scale)):
        weights[k * rank : (k + 1) * rank, :] = part
    swept = dot(image_table[:, :rank], image, NN, HIGHEST)
    distance, inverse = nearly_identity(swept)
    hold[...] = dot(inverse, swept, NN, HIGHEST)

    @pl.when(jnp.logical_not(distance <= 1e-5))
    def _():
        hold[...] = sweep(sweep(dot(factor, image, NN, HIGHEST)))

    basis[...] = hold[...]
    weights[3 * rank : 4 * rank, :] = hold[...].astype(BF16)

    sends = []
    for k, (start, stop) in enumerate(plan):
        fetches[k].wait()
        columns = slice(start, stop)
        out = dot(weights[...], held[start:stop, :], NT)
        left_held[:, columns] = (out[2 * rank : 3 * rank] + out[rank : 2 * rank]) + out[:rank]
        codes_held[:, columns] = out[3 * rank :].astype(BF16)
        span = pl.ds(start, stop - start)
        for q, (source, target) in enumerate(((left_held, left), (codes_held, codes))):
            copy = pltpu.make_async_copy(source.at[:, span], target.at[:, span], gone.at[q, k])
            copy.start()
            sends.append(copy)
    for copy in sends:
        copy.wait()


def finish(mine, other, sketch_rows, features, scale, core_of, weights=(5, 1)):
    rank, width = sketch_rows.shape
    rows = features.shape[0]
    plan = cuts(rows, weights)
    vmem = pl.BlockSpec(memory_space=pltpu.VMEM)
    hbm = pl.BlockSpec(memory_space=pl.ANY)
    return pl.pallas_call(
        functools.partial(finish_kernel, scale, plan, core_of),
        out_shape=(
            jax.ShapeDtypeStruct((rank, width), F32),
            jax.ShapeDtypeStruct((rank, rows), F32),
            jax.ShapeDtypeStruct((rank, rows), BF16),
        ),
        in_specs=[vmem, vmem, vmem, hbm],
        out_specs=(vmem, hbm, hbm),
        scratch_shapes=[
            pltpu.VMEM((3, width, width), BF16),
            pltpu.VMEM((rank, 2 * rank), F32),
            pltpu.VMEM((rank, 2 * rank), F32),
            pltpu.VMEM((rank, width), F32),
            pltpu.VMEM((4 * rank, width), BF16),
            pltpu.VMEM((rows, width), BF16),
            pltpu.VMEM((rank, rows), F32),
            pltpu.VMEM((rank, rows), BF16),
            pltpu.SemaphoreType.DMA((len(plan),)),
            pltpu.SemaphoreType.DMA((2, len(plan))),
        ],
        compiler_params=pltpu.CompilerParams(vmem_limit_bytes=ROOM),
        name="finish",
    )(mine, other, sketch_rows, pltpu.with_memory_space_constraint(features, pltpu.HBM))


def exchange(parts, axes):
    return lax.all_to_all(parts, axes, split_axis=0, concat_axis=0, tiled=True)


def swap(x):
    return lax.ppermute(x, "c", [(0, 1), (1, 0)])


def sum_everywhere(keep, send):
    slab, line = ("gx", "near"), "far"
    cells, length = lax.axis_size(slab), lax.axis_size(line)
    half = keep + swap(send)
    rows, width = half.shape
    share = jnp.sum(exchange(half.reshape(cells, rows // cells, 1, width), slab), axis=0)
    share = jnp.sum(exchange(jnp.broadcast_to(share, (length, *share.shape)), line), axis=0)
    mine = exchange(jnp.broadcast_to(share, (cells, *share.shape)), slab).reshape(rows, width)
    return mine, swap(mine)


def core_index():
    return lax.axis_index("c")


def on_device(features, sketch):
    scale = math.sqrt(features.shape[0] * lax.axis_size(("gx", "far", "near", "c")))
    mine, other = sum_everywhere(*local_gram(features, core_index))
    basis, left, codes = finish(mine, other, sketch.T, features, scale, core_index)
    return (basis.T, codes.T, left.T)


def solution(mesh):
    rows, columns = mesh.devices.shape
    mesh = Mesh(mesh.devices.reshape(rows, columns // 4, 2, 2), ("gx", "far", "near", "c"))
    split = P(("gx", "far", "near", "c"), None)
    return jax.shard_map(
        on_device,
        mesh=mesh,
        in_specs=(split, P()),
        out_specs=(P(), split, split),
        check_vma=False,
    )
```

```python
import functools
import math

import jax
import jax.numpy as jnp
from jax import lax
from jax.experimental import pallas as pl
from jax.experimental.pallas import tpu as pltpu
from jax.sharding import Mesh, PartitionSpec as P

BLOCK = 128
ROOM = 24 * 1024 * 1024
HIGHEST = lax.Precision.HIGHEST
PANEL = 8
NEAR = 1e-5
F32 = jnp.float32
BF16 = jnp.bfloat16
NT = (((1,), (1,)), ((), ()))
NN = (((1,), (0,)), ((), ()))
TN = (((0,), (0,)), ((), ()))


def dot(a, b, dims=NN, precision=None):
    return lax.dot_general(a, b, dims, precision=precision, preferred_element_type=F32)


def split3(x):
    high = x.astype(BF16)
    rest = x - high.astype(F32)
    middle = rest.astype(BF16)
    low = (rest - middle.astype(F32)).astype(BF16)
    return high, middle, low


def split2(x):
    high = x.astype(BF16)
    return high, (x - high.astype(F32)).astype(BF16)


def layout(n):
    pairs = [(i, j) for i in range(n) for j in range(i + 1, n)]
    count = len(pairs) // 2
    return (pairs[:count], (0, 1)), (pairs[count:], (2, 3))


def cuts(rows, weights):
    units = rows // BLOCK
    total = sum(weights)
    edges = [0]
    for k in range(len(weights)):
        edges.append(round(units * sum(weights[: k + 1]) / total) * BLOCK)
    return list(zip(edges[:-1], edges[1:]))


def gram_kernel(plan, core_of, features, keep, send, held, top, bottom, arrived):
    width = features.shape[1]
    n = width // BLOCK
    half = width // 2
    copies = []
    for k, (start, stop) in enumerate(plan):
        rows = pl.ds(start, stop - start)
        copy = pltpu.make_async_copy(features.at[rows], held.at[rows], arrived.at[k])
        copy.start()
        copies.append(copy)
    core = core_of()

    def add(k):
        start, stop = plan[k]
        copies[k].wait()
        f = held[start:stop, :]
        a = dot(f[:, :half], f, TN)
        b = dot(f[:, half:], f[:, half:], TN)
        top[...] = top[...] + a if k else a
        bottom[...] = bottom[...] + b if k else b

    for k in range(len(plan) - 1):
        pl.when(core >= 0)(functools.partial(add, k))
    add(len(plan) - 1)

    def block(i, j):
        if i >= n // 2:
            src, i, j = bottom, i - n // 2, j - n // 2
        else:
            src = top
        return src[i * BLOCK : (i + 1) * BLOCK, j * BLOCK : (j + 1) * BLOCK]

    halves = []
    for pairs, (a, b) in layout(n):
        low = lax.broadcasted_iota(jnp.int32, (BLOCK // 2, BLOCK), 1) < BLOCK // 2
        first, second = block(a, a), block(b, b)
        corner = pltpu.roll(first[BLOCK // 2 :], BLOCK // 2, 1)
        corners = jnp.where(low, corner, second[BLOCK // 2 :])
        halves.append(
            [block(*pair) for pair in pairs]
            + [first[: BLOCK // 2], second[: BLOCK // 2], corners]
        )
    at = 0
    for zero, one in zip(*halves):
        rows = slice(at, at + zero.shape[0])
        keep[rows, :] = jnp.where(core == 0, zero, one)
        send[rows, :] = jnp.where(core == 0, one, zero)
        at += zero.shape[0]


def local_gram(features, core_of, weights=(1, 2)):
    rows, width = features.shape
    n = width // BLOCK
    half = jax.ShapeDtypeStruct((n * (2 * n + 1) * BLOCK // 8, BLOCK), F32)
    plan = cuts(rows, weights)
    return pl.pallas_call(
        functools.partial(gram_kernel, plan, core_of),
        out_shape=(half, half),
        in_specs=[pl.BlockSpec(memory_space=pl.ANY)],
        out_specs=(pl.BlockSpec(memory_space=pltpu.VMEM),) * 2,
        scratch_shapes=[
            pltpu.VMEM((rows, width), BF16),
            pltpu.VMEM((width // 2, width), F32),
            pltpu.VMEM((width // 2, width // 2), F32),
            pltpu.SemaphoreType.DMA((len(plan),)),
        ],
        compiler_params=pltpu.CompilerParams(vmem_limit_bytes=ROOM),
        cost_estimate=pl.CostEstimate(
            flops=2 * rows * width * width, bytes_accessed=2 * rows * width, transcendentals=0
        ),
        name="gram",
    )(pltpu.with_memory_space_constraint(features, pltpu.HBM))


def beside_identity(gram, rank):
    lane = lax.broadcasted_iota(jnp.int32, (rank, 2 * rank), 1)
    row = lax.broadcasted_iota(jnp.int32, (rank, 2 * rank), 0)
    return gram + (lane == row).astype(F32)


def gram_of(a, b):
    both = jnp.concatenate([jnp.zeros_like(b), b], axis=0)
    return beside_identity(dot(a, both, NT, HIGHEST), a.shape[0])


def eliminate(tables, outs):
    rank, width = tables[0].shape
    rests = list(tables)
    for p in range(0, rank, PANEL):
        high = rank - p
        panels = [
            [
                jnp.broadcast_to(rest[:, rank + p + j : rank + p + j + 1], (high, width))
                for j in range(PANEL)
            ]
            for rest in rests
        ]
        for j in range(PANEL):
            for t, out in enumerate(outs):
                columns, rest = panels[t], rests[t]
                column = columns[j]
                pivot = column[j : j + 1, :]
                inverse = 1.0 / pivot
                row = rest[j : j + 1, :]
                out[p + j : p + j + 1, :] = row * lax.rsqrt(pivot)
                for i in range(j + 1, PANEL):
                    columns[i] = columns[i] - column * (columns[i][j : j + 1, :] * inverse)
                rests[t] = rest - column * (row * inverse)
        rests = [rest[PANEL:, :] for rest in rests]


def eliminate_slowly(gram, table, out):
    rank, width = gram.shape
    table[...] = gram
    lane = lax.broadcasted_iota(jnp.int32, (rank, width), 1)

    def step(k, carry):
        rest = table[...]
        column = jnp.sum(jnp.where(lane == rank + k, rest, 0.0), axis=1, keepdims=True)
        row = table[pl.ds(k, 1), :]
        pivot = jnp.sum(jnp.where(lane[:1] == rank + k, row, 0.0), axis=1, keepdims=True)
        out[pl.ds(k, 1), :] = row * lax.rsqrt(pivot)
        table[...] = rest - column * (row * (1.0 / pivot))
        return carry

    lax.fori_loop(0, rank, step, 0)


def polish(rows):
    rank = rows.shape[0]
    lane = lax.broadcasted_iota(jnp.int32, (rank, rank), 1)
    row = lax.broadcasted_iota(jnp.int32, (rank, rank), 0)
    eye = (lane == row).astype(F32)
    half = jnp.where(lane < row, 1.0, 0.0) + 0.5 * eye
    off = dot(rows, rows, NT, HIGHEST) - eye
    first = off * half
    rough = first.astype(BF16)
    change = (dot(rough, rough) + dot(rough, rough, NT) * half) - first
    high, low = split2(change)
    top, rest = split2(rows)
    return jnp.sum(off * off), rows + ((dot(low, top) + dot(high, rest)) + dot(high, top))


def finish_kernel(
    scale, plan, core_of, mine, other, sketch, features, basis, left, codes,
    parts, table, image_table, hold, weights, held, left_held, codes_held, arrived, gone,
):
    rank, width = sketch.shape
    n = width // BLOCK
    fetches = []
    for k, (start, stop) in enumerate(plan):
        rows = pl.ds(start, stop - start)
        copy = pltpu.make_async_copy(features.at[rows], held.at[rows], arrived.at[k])
        copy.start()
        fetches.append(copy)
    core = core_of()

    def store(i, j, block):
        for q, part in enumerate(split3(block)):
            parts[q, i * BLOCK : (i + 1) * BLOCK, j * BLOCK : (j + 1) * BLOCK] = part

    for half, (pairs, diagonal) in enumerate(layout(n)):

        def rows_at(start, size):
            rows = slice(start, start + size)
            return jnp.where(core == half, mine[rows, :], other[rows, :])

        for k, (i, j) in enumerate(pairs):
            block = rows_at(k * BLOCK, BLOCK)
            store(i, j, block)
            store(j, i, block.T)
        at = len(pairs) * BLOCK
        corners = rows_at(at + BLOCK, BLOCK // 2)
        for k, i in enumerate(diagonal):
            corner = corners if k else pltpu.roll(corners, BLOCK // 2, 1)
            block = jnp.concatenate([rows_at(at + k * BLOCK // 2, BLOCK // 2), corner], axis=0)
            lane = lax.broadcasted_iota(jnp.int32, (BLOCK, BLOCK), 1)
            row = lax.broadcasted_iota(jnp.int32, (BLOCK, BLOCK), 0)
            store(i, i, jnp.where((row >= BLOCK // 2) & (lane < BLOCK // 2), block.T, block))

    def times_gram(rows):
        return (dot(rows, parts[2]) + dot(rows, parts[1])) + dot(rows, parts[0])

    def sweep(rows):
        eliminate([gram_of(rows, rows)], [table])
        return dot(table[:, :rank], rows, NN, HIGHEST)

    def scale_left(factor, near):
        for k, part in enumerate(split2(dot(factor, near, NN, HIGHEST) * scale)):
            weights[k * rank : (k + 1) * rank, :] = part

    raw = times_gram(sketch[...])
    wide = sweep(raw)
    distance, polished = polish(wide)
    estimate = polished.astype(BF16)
    near = estimate.astype(F32)
    image = times_gram(estimate)
    eliminate([gram_of(image, near), gram_of(image, image)], [table, image_table])
    scale_left(table[:, :rank], near)
    swept = dot(image_table[:, :rank], image, NN, HIGHEST)
    distance_too, polished = polish(swept)
    hold[...] = polished

    @pl.when(jnp.logical_not(distance + distance_too <= NEAR))
    def _():
        def slow_sweep(rows):
            eliminate_slowly(gram_of(rows, rows), image_table, table)
            return dot(table[:, :rank], rows, NN, HIGHEST)

        estimate = slow_sweep(wide).astype(BF16)
        near = estimate.astype(F32)
        image = times_gram(estimate)
        eliminate_slowly(gram_of(image, near), image_table, table)
        factor = table[:, :rank]
        scale_left(factor, near)
        hold[...] = dot(factor, image, NN, HIGHEST)

        def again(k, carry):
            hold[...] = slow_sweep(hold[...])
            return carry

        lax.fori_loop(0, 2, again, 0)

    basis[...] = hold[...]
    weights[2 * rank : 3 * rank, :] = hold[...].astype(BF16)

    sends = []
    for k, (start, stop) in enumerate(plan):
        span = pl.ds(start, stop - start)
        own = [
            pltpu.make_async_copy(source.at[:, span], target.at[:, span], gone.at[q, k])
            for q, (source, target) in enumerate(((left_held, left), (codes_held, codes)))
        ]
        sends += own

        def piece(k=k, start=start, stop=stop, own=own):
            fetches[k].wait()
            columns = slice(start, stop)
            out = dot(weights[...], held[start:stop, :], NT)
            left_held[:, columns] = out[rank : 2 * rank] + out[:rank]
            codes_held[:, columns] = out[2 * rank :].astype(BF16)
            for copy in own:
                copy.start()

        pl.when(core >= 0)(piece)
    for copy in sends:
        copy.wait()


def finish(mine, other, sketch_rows, features, scale, core_of, weights=(5, 1)):
    rank, width = sketch_rows.shape
    rows = features.shape[0]
    plan = cuts(rows, weights)
    vmem = pl.BlockSpec(memory_space=pltpu.VMEM)
    hbm = pl.BlockSpec(memory_space=pl.ANY)
    return pl.pallas_call(
        functools.partial(finish_kernel, scale, plan, core_of),
        out_shape=(
            jax.ShapeDtypeStruct((rank, width), F32),
            jax.ShapeDtypeStruct((rank, rows), F32),
            jax.ShapeDtypeStruct((rank, rows), BF16),
        ),
        in_specs=[vmem, vmem, vmem, hbm],
        out_specs=(vmem, hbm, hbm),
        scratch_shapes=[
            pltpu.VMEM((3, width, width), BF16),
            pltpu.VMEM((rank, 2 * rank), F32),
            pltpu.VMEM((rank, 2 * rank), F32),
            pltpu.VMEM((rank, width), F32),
            pltpu.VMEM((3 * rank, width), BF16),
            pltpu.VMEM((rows, width), BF16),
            pltpu.VMEM((rank, rows), F32),
            pltpu.VMEM((rank, rows), BF16),
            pltpu.SemaphoreType.DMA((len(plan),)),
            pltpu.SemaphoreType.DMA((2, len(plan))),
        ],
        compiler_params=pltpu.CompilerParams(vmem_limit_bytes=ROOM),
        name="finish",
    )(mine, other, sketch_rows, pltpu.with_memory_space_constraint(features, pltpu.HBM))


def exchange(parts, axes):
    return lax.all_to_all(parts, axes, split_axis=0, concat_axis=0, tiled=True)


def swap(x):
    return lax.ppermute(x, "c", [(0, 1), (1, 0)])


def sum_everywhere(keep, send):
    slab, line = ("gx", "near"), "far"
    cells, length = lax.axis_size(slab), lax.axis_size(line)
    half = keep + swap(send)
    rows, width = half.shape
    share = jnp.sum(exchange(half.reshape(cells, rows // cells, 1, width), slab), axis=0)
    share = jnp.sum(exchange(jnp.broadcast_to(share, (length, *share.shape)), line), axis=0)
    mine = exchange(jnp.broadcast_to(share, (cells, *share.shape)), slab).reshape(rows, width)
    return mine, swap(mine)


def core_index():
    return lax.axis_index("c")


def on_device(features, sketch):
    scale = math.sqrt(features.shape[0] * lax.axis_size(("gx", "far", "near", "c")))
    mine, other = sum_everywhere(*local_gram(features, core_index))
    basis, left, codes = finish(mine, other, sketch.T, features, scale, core_index)
    return (basis.T, codes.T, left.T)


def solution(mesh):
    rows, columns = mesh.devices.shape
    mesh = Mesh(mesh.devices.reshape(rows, columns // 4, 2, 2), ("gx", "far", "near", "c"))
    split = P(("gx", "far", "near", "c"), None)
    return jax.shard_map(
        on_device,
        mesh=mesh,
        in_specs=(split, P()),
        out_specs=(P(), split, split),
        check_vma=False,
    )
```

```python
import functools
import math

import jax
import jax.numpy as jnp
from jax import lax
from jax.experimental import pallas as pl
from jax.experimental.pallas import tpu as pltpu
from jax.sharding import Mesh, PartitionSpec as P

BLOCK = 128
ROOM = 24 * 1024 * 1024
HIGHEST = lax.Precision.HIGHEST
NEAR = 1e-5
F32 = jnp.float32
BF16 = jnp.bfloat16
NT = (((1,), (1,)), ((), ()))
NN = (((1,), (0,)), ((), ()))
TN = (((0,), (0,)), ((), ()))


def dot(a, b, dims=NN, precision=None):
    return lax.dot_general(a, b, dims, precision=precision, preferred_element_type=F32)


def split3(x):
    high = x.astype(BF16)
    rest = x - high.astype(F32)
    middle = rest.astype(BF16)
    low = (rest - middle.astype(F32)).astype(BF16)
    return high, middle, low


def split2(x):
    high = x.astype(BF16)
    return high, (x - high.astype(F32)).astype(BF16)


def layout(n):
    pairs = [(i, j) for i in range(n) for j in range(i + 1, n)]
    count = len(pairs) // 2
    return (pairs[:count], (0, 1)), (pairs[count:], (2, 3))


def cuts(rows, weights):
    units = rows // BLOCK
    total = sum(weights)
    edges = [0]
    for k in range(len(weights)):
        edges.append(round(units * sum(weights[: k + 1]) / total) * BLOCK)
    return list(zip(edges[:-1], edges[1:]))


def gram_kernel(plan, core_of, features, keep, send, held, top, bottom, arrived):
    width = features.shape[1]
    n = width // BLOCK
    half = width // 2
    copies = []
    for k, (start, stop) in enumerate(plan):
        rows = pl.ds(start, stop - start)
        copy = pltpu.make_async_copy(features.at[rows], held.at[rows], arrived.at[k])
        copy.start()
        copies.append(copy)
    core = core_of()

    def add(k):
        start, stop = plan[k]
        copies[k].wait()
        f = held[start:stop, :]
        a = dot(f[:, :half], f, TN)
        b = dot(f[:, half:], f[:, half:], TN)
        top[...] = top[...] + a if k else a
        bottom[...] = bottom[...] + b if k else b

    for k in range(len(plan) - 1):
        pl.when(core >= 0)(functools.partial(add, k))
    add(len(plan) - 1)

    def block(i, j):
        if i >= n // 2:
            src, i, j = bottom, i - n // 2, j - n // 2
        else:
            src = top
        return src[i * BLOCK : (i + 1) * BLOCK, j * BLOCK : (j + 1) * BLOCK]

    halves = []
    for pairs, (a, b) in layout(n):
        low = lax.broadcasted_iota(jnp.int32, (BLOCK // 2, BLOCK), 1) < BLOCK // 2
        first, second = block(a, a), block(b, b)
        corner = pltpu.roll(first[BLOCK // 2 :], BLOCK // 2, 1)
        corners = jnp.where(low, corner, second[BLOCK // 2 :])
        halves.append(
            [block(*pair) for pair in pairs]
            + [first[: BLOCK // 2], second[: BLOCK // 2], corners]
        )
    at = 0
    for zero, one in zip(*halves):
        rows = slice(at, at + zero.shape[0])
        keep[rows, :] = jnp.where(core == 0, zero, one)
        send[rows, :] = jnp.where(core == 0, one, zero)
        at += zero.shape[0]


def local_gram(features, core_of, weights=(1, 2)):
    rows, width = features.shape
    n = width // BLOCK
    half = jax.ShapeDtypeStruct((n * (2 * n + 1) * BLOCK // 8, BLOCK), F32)
    plan = cuts(rows, weights)
    return pl.pallas_call(
        functools.partial(gram_kernel, plan, core_of),
        out_shape=(half, half),
        in_specs=[pl.BlockSpec(memory_space=pl.ANY)],
        out_specs=(pl.BlockSpec(memory_space=pltpu.VMEM),) * 2,
        scratch_shapes=[
            pltpu.VMEM((rows, width), BF16),
            pltpu.VMEM((width // 2, width), F32),
            pltpu.VMEM((width // 2, width // 2), F32),
            pltpu.SemaphoreType.DMA((len(plan),)),
        ],
        compiler_params=pltpu.CompilerParams(vmem_limit_bytes=ROOM),
        cost_estimate=pl.CostEstimate(
            flops=2 * rows * width * width, bytes_accessed=2 * rows * width, transcendentals=0
        ),
        name="gram",
    )(pltpu.with_memory_space_constraint(features, pltpu.HBM))


def beside_identity(gram, rank):
    lane = lax.broadcasted_iota(jnp.int32, (rank, 2 * rank), 1)
    row = lax.broadcasted_iota(jnp.int32, (rank, 2 * rank), 0)
    return gram + (lane == row).astype(F32)


def gram_of(a, b):
    both = jnp.concatenate([jnp.zeros_like(b), b], axis=0)
    return beside_identity(dot(a, both, NT, HIGHEST), a.shape[0])


def eliminate(tables, outs):
    rank, width = tables[0].shape
    rests = list(tables)

    def spread(rest, skip, at):
        high = rest.shape[0] - skip
        return [
            jnp.broadcast_to(rest[skip:, at + j : at + j + 1], (high, width)) for j in range(8)
        ]

    panels = [spread(rest, 0, rank) for rest in rests]
    for p in range(0, rank, 8):
        last = p + 8 == rank
        look = len(outs) == 1
        ahead = [[] if last or not look else spread(rest, 8, rank + p + 8) for rest in rests]
        for j in range(8):
            for t, out in enumerate(outs):
                columns, rest = panels[t], rests[t]
                column = columns[j]
                pivot = column[j : j + 1, :]
                inverse = 1.0 / pivot
                row = rest[j : j + 1, :]
                out[p + j : p + j + 1, :] = row * lax.rsqrt(pivot)
                for i in range(j + 1, 8):
                    columns[i] = columns[i] - column * (column[i : i + 1, :] * inverse)
                for i in range(len(ahead[t])):
                    factor = column[8 + i : 9 + i, :] * inverse
                    ahead[t][i] = ahead[t][i] - column[8:, :] * factor
                rests[t] = rest - column * (row * inverse)
        rests = [rest[8:, :] for rest in rests]
        if not last:
            panels = ahead if look else [spread(rest, 0, rank + p + 8) for rest in rests]


def eliminate_slowly(gram, table, out):
    rank, width = gram.shape
    table[...] = gram
    lane = lax.broadcasted_iota(jnp.int32, (rank, width), 1)

    def step(k, carry):
        rest = table[...]
        column = jnp.sum(jnp.where(lane == rank + k, rest, 0.0), axis=1, keepdims=True)
        row = table[pl.ds(k, 1), :]
        pivot = jnp.sum(jnp.where(lane[:1] == rank + k, row, 0.0), axis=1, keepdims=True)
        out[pl.ds(k, 1), :] = row * lax.rsqrt(pivot)
        table[...] = rest - column * (row * (1.0 / pivot))
        return carry

    lax.fori_loop(0, rank, step, 0)


def polish(rows):
    rank = rows.shape[0]
    lane = lax.broadcasted_iota(jnp.int32, (rank, rank), 1)
    row = lax.broadcasted_iota(jnp.int32, (rank, rank), 0)
    eye = (lane == row).astype(F32)
    half = jnp.where(lane < row, 1.0, 0.0) + 0.5 * eye
    off = dot(rows, rows, NT, HIGHEST) - eye
    first = off * half
    rough = first.astype(BF16)
    change = (dot(rough, rough) + dot(rough, rough, NT) * half) - first
    high, low = split2(change)
    top, rest = split2(rows)
    return jnp.sum(off * off), rows + ((dot(low, top) + dot(high, rest)) + dot(high, top))


def finish_kernel(
    scale, plan, core_of, mine, other, sketch, features, basis, left, codes,
    parts, table, image_table, hold, weights, held, left_held, codes_held, arrived, gone, done,
):
    rank, width = sketch.shape
    n = width // BLOCK
    fetches = []
    for k, (start, stop) in enumerate(plan):
        rows = pl.ds(start, stop - start)
        copy = pltpu.make_async_copy(features.at[rows], held.at[rows], arrived.at[k])
        copy.start()
        fetches.append(copy)
    core = core_of()

    def store(i, j, block):
        for q, part in enumerate(split3(block)):
            parts[q, i * BLOCK : (i + 1) * BLOCK, j * BLOCK : (j + 1) * BLOCK] = part

    for half, (pairs, diagonal) in enumerate(layout(n)):

        def rows_at(start, size):
            rows = slice(start, start + size)
            return jnp.where(core == half, mine[rows, :], other[rows, :])

        for k, (i, j) in enumerate(pairs):
            block = rows_at(k * BLOCK, BLOCK)
            store(i, j, block)
            store(j, i, block.T)
        at = len(pairs) * BLOCK
        corners = rows_at(at + BLOCK, BLOCK // 2)
        for k, i in enumerate(diagonal):
            corner = corners if k else pltpu.roll(corners, BLOCK // 2, 1)
            block = jnp.concatenate([rows_at(at + k * BLOCK // 2, BLOCK // 2), corner], axis=0)
            lane = lax.broadcasted_iota(jnp.int32, (BLOCK, BLOCK), 1)
            row = lax.broadcasted_iota(jnp.int32, (BLOCK, BLOCK), 0)
            store(i, i, jnp.where((row >= BLOCK // 2) & (lane < BLOCK // 2), block.T, block))

    def times_gram(rows):
        return (dot(rows, parts[2]) + dot(rows, parts[1])) + dot(rows, parts[0])

    def sweep(rows):
        eliminate([gram_of(rows, rows)], [table])
        return dot(table[:, :rank], rows, NN, HIGHEST)

    def scale_left(factor, near):
        for k, part in enumerate(split2(dot(factor, near, NN, HIGHEST) * scale)):
            weights[k * rank : (k + 1) * rank, :] = part

    raw = times_gram(sketch[...])
    wide = sweep(raw)
    distance, polished = polish(wide)
    estimate = polished.astype(BF16)
    near = estimate.astype(F32)
    image = times_gram(estimate)
    eliminate([gram_of(image, near), gram_of(image, image)], [table, image_table])
    scale_left(table[:, :rank], near)
    swept = dot(image_table[:, :rank], image, NN, HIGHEST)
    distance_too, polished = polish(swept)
    hold[...] = polished

    @pl.when(jnp.logical_not(distance + distance_too <= NEAR))
    def _():
        def slow_sweep(rows):
            eliminate_slowly(gram_of(rows, rows), image_table, table)
            return dot(table[:, :rank], rows, NN, HIGHEST)

        estimate = slow_sweep(wide).astype(BF16)
        near = estimate.astype(F32)
        image = times_gram(estimate)
        eliminate_slowly(gram_of(image, near), image_table, table)
        factor = table[:, :rank]
        scale_left(factor, near)
        hold[...] = dot(factor, image, NN, HIGHEST)

        def again(k, carry):
            hold[...] = slow_sweep(hold[...])
            return carry

        lax.fori_loop(0, 2, again, 0)

    own_copy = pltpu.make_async_copy(hold, basis, done)
    own_copy.start()
    weights[2 * rank : 3 * rank, :] = hold[...].astype(BF16)

    sends = [own_copy]
    for k, (start, stop) in enumerate(plan):
        span = pl.ds(start, stop - start)
        own = [
            pltpu.make_async_copy(source.at[:, span], target.at[:, span], gone.at[q, k])
            for q, (source, target) in enumerate(((left_held, left), (codes_held, codes)))
        ]
        sends += own

        def piece(k=k, start=start, stop=stop, own=own):
            fetches[k].wait()
            columns = slice(start, stop)
            out = dot(weights[...], held[start:stop, :], NT)
            left_held[:, columns] = out[rank : 2 * rank] + out[:rank]
            codes_held[:, columns] = out[2 * rank :].astype(BF16)
            for copy in own:
                copy.start()

        pl.when(core >= 0)(piece)
    for copy in sends:
        copy.wait()


def finish(mine, other, sketch_rows, features, scale, core_of, weights=(5, 1)):
    rank, width = sketch_rows.shape
    rows = features.shape[0]
    plan = cuts(rows, weights)
    vmem = pl.BlockSpec(memory_space=pltpu.VMEM)
    hbm = pl.BlockSpec(memory_space=pl.ANY)
    return pl.pallas_call(
        functools.partial(finish_kernel, scale, plan, core_of),
        out_shape=(
            jax.ShapeDtypeStruct((rank, width), F32),
            jax.ShapeDtypeStruct((rank, rows), F32),
            jax.ShapeDtypeStruct((rank, rows), BF16),
        ),
        in_specs=[vmem, vmem, vmem, hbm],
        out_specs=(hbm, hbm, hbm),
        scratch_shapes=[
            pltpu.VMEM((3, width, width), BF16),
            pltpu.VMEM((rank, 2 * rank), F32),
            pltpu.VMEM((rank, 2 * rank), F32),
            pltpu.VMEM((rank, width), F32),
            pltpu.VMEM((3 * rank, width), BF16),
            pltpu.VMEM((rows, width), BF16),
            pltpu.VMEM((rank, rows), F32),
            pltpu.VMEM((rank, rows), BF16),
            pltpu.SemaphoreType.DMA((len(plan),)),
            pltpu.SemaphoreType.DMA((2, len(plan))),
            pltpu.SemaphoreType.DMA(()),
        ],
        compiler_params=pltpu.CompilerParams(vmem_limit_bytes=ROOM),
        name="finish",
    )(mine, other, sketch_rows, pltpu.with_memory_space_constraint(features, pltpu.HBM))


def exchange(parts, axes):
    return lax.all_to_all(parts, axes, split_axis=0, concat_axis=0, tiled=True)


def swap(x):
    return lax.ppermute(x, "c", [(0, 1), (1, 0)])


def sum_everywhere(keep, send):
    slab, line = ("gx", "near"), "far"
    cells, length = lax.axis_size(slab), lax.axis_size(line)
    half = keep + swap(send)
    rows, width = half.shape
    share = jnp.sum(exchange(half.reshape(cells, rows // cells, 1, width), slab), axis=0)
    share = jnp.sum(exchange(jnp.broadcast_to(share, (length, *share.shape)), line), axis=0)
    mine = exchange(jnp.broadcast_to(share, (cells, *share.shape)), slab).reshape(rows, width)
    return mine, swap(mine)


def core_index():
    return lax.axis_index("c")


def on_device(features, sketch):
    scale = math.sqrt(features.shape[0] * lax.axis_size(("gx", "far", "near", "c")))
    mine, other = sum_everywhere(*local_gram(features, core_index))
    basis, left, codes = finish(mine, other, sketch.T, features, scale, core_index)
    return (basis.T, codes.T, left.T)


def solution(mesh):
    rows, columns = mesh.devices.shape
    mesh = Mesh(mesh.devices.reshape(rows, columns // 4, 2, 2), ("gx", "far", "near", "c"))
    split = P(("gx", "far", "near", "c"), None)
    return jax.shard_map(
        on_device,
        mesh=mesh,
        in_specs=(split, P()),
        out_specs=(P(), split, split),
        check_vma=False,
    )
```

```python
import functools
import math

import jax
import jax.numpy as jnp
from jax import lax
from jax.experimental import pallas as pl
from jax.experimental.pallas import tpu as pltpu
from jax.sharding import Mesh, PartitionSpec as P

BLOCK = 128
ROOM = 24 * 1024 * 1024
HIGHEST = lax.Precision.HIGHEST
NEAR = 1e-5
F32 = jnp.float32
BF16 = jnp.bfloat16
NT = (((1,), (1,)), ((), ()))
NN = (((1,), (0,)), ((), ()))
TN = (((0,), (0,)), ((), ()))


def dot(a, b, dims=NN, precision=None):
    return lax.dot_general(a, b, dims, precision=precision, preferred_element_type=F32)


def split3(x):
    high = x.astype(BF16)
    rest = x - high.astype(F32)
    middle = rest.astype(BF16)
    low = (rest - middle.astype(F32)).astype(BF16)
    return high, middle, low


def split2(x):
    high = x.astype(BF16)
    return high, (x - high.astype(F32)).astype(BF16)


def layout(n):
    pairs = [(i, j) for i in range(n) for j in range(i + 1, n)]
    count = len(pairs) // 2
    return (pairs[:count], (0, 1)), (pairs[count:], (2, 3))


def cuts(rows, weights):
    units = rows // BLOCK
    total = sum(weights)
    edges = [0]
    for k in range(len(weights)):
        edges.append(round(units * sum(weights[: k + 1]) / total) * BLOCK)
    return list(zip(edges[:-1], edges[1:]))


def gram_kernel(plan, core_of, features, keep, send, held, top, bottom, arrived):
    width = features.shape[1]
    n = width // BLOCK
    half = width // 2
    copies = []
    for k, (start, stop) in enumerate(plan):
        rows = pl.ds(start, stop - start)
        copy = pltpu.make_async_copy(features.at[rows], held.at[rows], arrived.at[k])
        copy.start()
        copies.append(copy)
    core = core_of()

    def add(k):
        start, stop = plan[k]
        copies[k].wait()
        f = held[start:stop, :]
        a = dot(f[:, :half], f, TN)
        b = dot(f[:, half:], f[:, half:], TN)
        top[...] = top[...] + a if k else a
        bottom[...] = bottom[...] + b if k else b

    for k in range(len(plan) - 1):
        pl.when(core >= 0)(functools.partial(add, k))
    add(len(plan) - 1)

    def block(i, j):
        if i >= n // 2:
            src, i, j = bottom, i - n // 2, j - n // 2
        else:
            src = top
        return src[i * BLOCK : (i + 1) * BLOCK, j * BLOCK : (j + 1) * BLOCK]

    halves = []
    for pairs, (a, b) in layout(n):
        low = lax.broadcasted_iota(jnp.int32, (BLOCK // 2, BLOCK), 1) < BLOCK // 2
        first, second = block(a, a), block(b, b)
        corner = pltpu.roll(first[BLOCK // 2 :], BLOCK // 2, 1)
        corners = jnp.where(low, corner, second[BLOCK // 2 :])
        halves.append(
            [block(*pair) for pair in pairs]
            + [first[: BLOCK // 2], second[: BLOCK // 2], corners]
        )
    at = 0
    for zero, one in zip(*halves):
        rows = slice(at, at + zero.shape[0])
        keep[rows, :] = jnp.where(core == 0, zero, one)
        send[rows, :] = jnp.where(core == 0, one, zero)
        at += zero.shape[0]


def local_gram(features, core_of, weights=(1, 2)):
    rows, width = features.shape
    n = width // BLOCK
    half = jax.ShapeDtypeStruct((n * (2 * n + 1) * BLOCK // 8, BLOCK), F32)
    plan = cuts(rows, weights)
    return pl.pallas_call(
        functools.partial(gram_kernel, plan, core_of),
        out_shape=(half, half),
        in_specs=[pl.BlockSpec(memory_space=pl.ANY)],
        out_specs=(pl.BlockSpec(memory_space=pltpu.VMEM),) * 2,
        scratch_shapes=[
            pltpu.VMEM((rows, width), BF16),
            pltpu.VMEM((width // 2, width), F32),
            pltpu.VMEM((width // 2, width // 2), F32),
            pltpu.SemaphoreType.DMA((len(plan),)),
        ],
        compiler_params=pltpu.CompilerParams(vmem_limit_bytes=ROOM),
        cost_estimate=pl.CostEstimate(
            flops=2 * rows * width * width, bytes_accessed=2 * rows * width, transcendentals=0
        ),
        name="gram",
    )(pltpu.with_memory_space_constraint(features, pltpu.HBM))


def beside_identity(gram, rank):
    lane = lax.broadcasted_iota(jnp.int32, (rank, 2 * rank), 1)
    row = lax.broadcasted_iota(jnp.int32, (rank, 2 * rank), 0)
    return gram + (lane == row).astype(F32)


def gram_of(a, b):
    both = jnp.concatenate([jnp.zeros_like(b), b], axis=0)
    return beside_identity(dot(a, both, NT, HIGHEST), a.shape[0])


def eliminate(tables, outs):
    rank, width = tables[0].shape
    rests = list(tables)

    def spread(rest, skip, at):
        high = rest.shape[0] - skip
        return [
            jnp.broadcast_to(rest[skip:, at + j : at + j + 1], (high, width)) for j in range(8)
        ]

    panels = [spread(rest, 0, rank) for rest in rests]
    for p in range(0, rank, 8):
        last = p + 8 == rank
        look = len(outs) == 1
        ahead = [[] if last or not look else spread(rest, 8, rank + p + 8) for rest in rests]
        for j in range(8):
            for t, out in enumerate(outs):
                columns, rest = panels[t], rests[t]
                column = columns[j]
                pivot = column[j : j + 1, :]
                inverse = 1.0 / pivot
                row = rest[j : j + 1, :]
                out[p + j : p + j + 1, :] = row * lax.rsqrt(pivot)
                for i in range(j + 1, 8):
                    columns[i] = columns[i] - column * (column[i : i + 1, :] * inverse)
                for i in range(len(ahead[t])):
                    factor = column[8 + i : 9 + i, :] * inverse
                    ahead[t][i] = ahead[t][i] - column[8:, :] * factor
                rests[t] = rest - column * (row * inverse)
        rests = [rest[8:, :] for rest in rests]
        if not last:
            panels = ahead if look else [spread(rest, 0, rank + p + 8) for rest in rests]


def eliminate_slowly(gram, table, out):
    rank, width = gram.shape
    table[...] = gram
    lane = lax.broadcasted_iota(jnp.int32, (rank, width), 1)

    def step(k, carry):
        rest = table[...]
        column = jnp.sum(jnp.where(lane == rank + k, rest, 0.0), axis=1, keepdims=True)
        row = table[pl.ds(k, 1), :]
        pivot = jnp.sum(jnp.where(lane[:1] == rank + k, row, 0.0), axis=1, keepdims=True)
        out[pl.ds(k, 1), :] = row * lax.rsqrt(pivot)
        table[...] = rest - column * (row * (1.0 / pivot))
        return carry

    lax.fori_loop(0, rank, step, 0)


def polish(rows):
    rank = rows.shape[0]
    lane = lax.broadcasted_iota(jnp.int32, (rank, rank), 1)
    row = lax.broadcasted_iota(jnp.int32, (rank, rank), 0)
    eye = (lane == row).astype(F32)
    half = jnp.where(lane < row, 1.0, 0.0) + 0.5 * eye
    off = dot(rows, rows, NT, HIGHEST) - eye
    first = off * half
    rough = first.astype(BF16)
    change = (dot(rough, rough) + dot(rough, rough, NT) * half) - first
    high, low = split2(change)
    top, rest = split2(rows)
    return jnp.sum(off * off), rows + ((dot(low, top) + dot(high, rest)) + dot(high, top))


def finish_kernel(
    scale, plan, core_of, mine, other, sketch, features, basis, left, codes,
    parts, table, image_table, hold, weights, held, left_held, codes_held, arrived, gone, done,
):
    rank, width = sketch.shape
    n = width // BLOCK
    fetches = []
    for k, (start, stop) in enumerate(plan):
        rows = pl.ds(start, stop - start)
        copy = pltpu.make_async_copy(features.at[rows], held.at[rows], arrived.at[k])
        copy.start()
        fetches.append(copy)
    core = core_of()

    def store(i, j, block):
        for q, part in enumerate(split3(block)):
            parts[q, i * BLOCK : (i + 1) * BLOCK, j * BLOCK : (j + 1) * BLOCK] = part

    for half, (pairs, diagonal) in enumerate(layout(n)):

        def rows_at(start, size):
            rows = slice(start, start + size)
            return jnp.where(core == half, mine[rows, :], other[rows, :])

        for k, (i, j) in enumerate(pairs):
            block = rows_at(k * BLOCK, BLOCK)
            store(i, j, block)
            store(j, i, block.T)
        at = len(pairs) * BLOCK
        corners = rows_at(at + BLOCK, BLOCK // 2)
        for k, i in enumerate(diagonal):
            corner = corners if k else pltpu.roll(corners, BLOCK // 2, 1)
            block = jnp.concatenate([rows_at(at + k * BLOCK // 2, BLOCK // 2), corner], axis=0)
            lane = lax.broadcasted_iota(jnp.int32, (BLOCK, BLOCK), 1)
            row = lax.broadcasted_iota(jnp.int32, (BLOCK, BLOCK), 0)
            store(i, i, jnp.where((row >= BLOCK // 2) & (lane < BLOCK // 2), block.T, block))

    def times_gram(rows):
        return (dot(rows, parts[2]) + dot(rows, parts[1])) + dot(rows, parts[0])

    def sweep(rows):
        eliminate([gram_of(rows, rows)], [table])
        return dot(table[:, :rank], rows, NN, HIGHEST)

    def scale_left(factor, near):
        for k, part in enumerate(split2(dot(factor, near, NN, HIGHEST) * scale)):
            weights[k * rank : (k + 1) * rank, :] = part

    raw = times_gram(sketch[...])
    wide = sweep(raw)
    distance, polished = polish(wide)
    estimate = polished.astype(BF16)
    near = estimate.astype(F32)
    image = times_gram(estimate)
    eliminate([gram_of(image, near), gram_of(image, image)], [table, image_table])
    scale_left(table[:, :rank], near)
    swept = dot(image_table[:, :rank], image, NN, HIGHEST)
    distance_too, polished = polish(swept)
    hold[...] = polished

    @pl.when(jnp.logical_not(distance + distance_too <= NEAR))
    def _():
        def slow_sweep(rows):
            eliminate_slowly(gram_of(rows, rows), image_table, table)
            return dot(table[:, :rank], rows, NN, HIGHEST)

        estimate = slow_sweep(wide).astype(BF16)
        near = estimate.astype(F32)
        image = times_gram(estimate)
        eliminate_slowly(gram_of(image, near), image_table, table)
        factor = table[:, :rank]
        scale_left(factor, near)
        hold[...] = dot(factor, image, NN, HIGHEST)

        def again(k, carry):
            hold[...] = slow_sweep(hold[...])
            return carry

        lax.fori_loop(0, 2, again, 0)

    own_copy = pltpu.make_async_copy(hold, basis, done)
    own_copy.start()
    weights[2 * rank : 3 * rank, :] = hold[...].astype(BF16)

    sends = [own_copy]
    for k, (start, stop) in enumerate(plan):
        span = pl.ds(start, stop - start)
        own = [
            pltpu.make_async_copy(source.at[:, span], target.at[:, span], gone.at[q, k])
            for q, (source, target) in enumerate(((left_held, left), (codes_held, codes)))
        ]
        sends += own

        def piece(k=k, start=start, stop=stop, own=own):
            fetches[k].wait()
            columns = slice(start, stop)
            out = dot(weights[...], held[start:stop, :], NT)
            left_held[:, columns] = out[rank : 2 * rank] + out[:rank]
            codes_held[:, columns] = out[2 * rank :].astype(BF16)
            for copy in own:
                copy.start()

        pl.when(core >= 0)(piece)
    for copy in sends:
        copy.wait()


def finish(mine, other, sketch_rows, features, scale, core_of, weights=(5, 1)):
    rank, width = sketch_rows.shape
    rows = features.shape[0]
    plan = cuts(rows, weights)
    vmem = pl.BlockSpec(memory_space=pltpu.VMEM)
    hbm = pl.BlockSpec(memory_space=pl.ANY)
    return pl.pallas_call(
        functools.partial(finish_kernel, scale, plan, core_of),
        out_shape=(
            jax.ShapeDtypeStruct((rank, width), F32),
            jax.ShapeDtypeStruct((rank, rows), F32),
            jax.ShapeDtypeStruct((rank, rows), BF16),
        ),
        in_specs=[vmem, vmem, vmem, hbm],
        out_specs=(hbm, hbm, hbm),
        scratch_shapes=[
            pltpu.VMEM((3, width, width), BF16),
            pltpu.VMEM((rank, 2 * rank), F32),
            pltpu.VMEM((rank, 2 * rank), F32),
            pltpu.VMEM((rank, width), F32),
            pltpu.VMEM((3 * rank, width), BF16),
            pltpu.VMEM((rows, width), BF16),
            pltpu.VMEM((rank, rows), F32),
            pltpu.VMEM((rank, rows), BF16),
            pltpu.SemaphoreType.DMA((len(plan),)),
            pltpu.SemaphoreType.DMA((2, len(plan))),
            pltpu.SemaphoreType.DMA(()),
        ],
        compiler_params=pltpu.CompilerParams(vmem_limit_bytes=ROOM),
        name="finish",
    )(mine, other, sketch_rows, pltpu.with_memory_space_constraint(features, pltpu.HBM))


def exchange(parts, axes):
    return lax.all_to_all(parts, axes, split_axis=0, concat_axis=0, tiled=True)


def swap(x):
    return lax.ppermute(x, "c", [(0, 1), (1, 0)])


def sum_everywhere(keep, send):
    slab, line = ("gx", "near"), "far"
    cells, length = lax.axis_size(slab), lax.axis_size(line)
    half = keep + swap(send)
    rows, width = half.shape
    pieces = half.reshape(cells, rows // cells // 2, 2, width)
    share = jnp.sum(exchange(pieces, slab), axis=0)
    share = jnp.sum(exchange(jnp.broadcast_to(share, (length, *share.shape)), line), axis=0)
    mine = exchange(jnp.broadcast_to(share, (cells, *share.shape)), slab).reshape(rows, width)
    return mine, swap(mine)


def core_index():
    return lax.axis_index("c")


def on_device(features, sketch):
    scale = math.sqrt(features.shape[0] * lax.axis_size(("gx", "far", "near", "c")))
    mine, other = sum_everywhere(*local_gram(features, core_index))
    basis, left, codes = finish(mine, other, sketch.T, features, scale, core_index)
    return (basis.T, codes.T, left.T)


def solution(mesh):
    rows, columns = mesh.devices.shape
    mesh = Mesh(mesh.devices.reshape(rows, columns // 4, 2, 2), ("gx", "far", "near", "c"))
    split = P(("gx", "far", "near", "c"), None)
    return jax.shard_map(
        on_device,
        mesh=mesh,
        in_specs=(split, P()),
        out_specs=(P(), split, split),
        check_vma=False,
    )
```

```python
import functools
import math

import jax
import jax.numpy as jnp
from jax import lax
from jax.experimental import pallas as pl
from jax.experimental.pallas import tpu as pltpu
from jax.sharding import Mesh, PartitionSpec as P

BLOCK = 128
ROOM = 24 * 1024 * 1024
HIGHEST = lax.Precision.HIGHEST
NEAR = 1e-5
F32 = jnp.float32
BF16 = jnp.bfloat16
NT = (((1,), (1,)), ((), ()))
NN = (((1,), (0,)), ((), ()))
TN = (((0,), (0,)), ((), ()))


def dot(a, b, dims=NN, precision=None):
    return lax.dot_general(a, b, dims, precision=precision, preferred_element_type=F32)


def split3(x):
    high = x.astype(BF16)
    rest = x - high.astype(F32)
    middle = rest.astype(BF16)
    low = (rest - middle.astype(F32)).astype(BF16)
    return high, middle, low


def split2(x):
    high = x.astype(BF16)
    return high, (x - high.astype(F32)).astype(BF16)


def layout(n):
    pairs = [(i, j) for i in range(n) for j in range(i + 1, n)]
    count = len(pairs) // 2
    return (pairs[:count], (0, 1)), (pairs[count:], (2, 3))


def cuts(rows, weights):
    units = rows // BLOCK
    total = sum(weights)
    edges = [0]
    for k in range(len(weights)):
        edges.append(round(units * sum(weights[: k + 1]) / total) * BLOCK)
    return list(zip(edges[:-1], edges[1:]))


def gram_kernel(plan, core_of, features, keep, send, held, top, bottom, arrived):
    width = features.shape[1]
    n = width // BLOCK
    half = width // 2
    copies = []
    for k, (start, stop) in enumerate(plan):
        rows = pl.ds(start, stop - start)
        copy = pltpu.make_async_copy(features.at[rows], held.at[rows], arrived.at[k])
        copy.start()
        copies.append(copy)
    core = core_of()

    def add(k):
        start, stop = plan[k]
        copies[k].wait()
        f = held[start:stop, :]
        a = dot(f[:, :half], f, TN)
        b = dot(f[:, half:], f[:, half:], TN)
        top[...] = top[...] + a if k else a
        bottom[...] = bottom[...] + b if k else b

    for k in range(len(plan) - 1):
        pl.when(core >= 0)(functools.partial(add, k))
    add(len(plan) - 1)

    def block(i, j):
        if i >= n // 2:
            src, i, j = bottom, i - n // 2, j - n // 2
        else:
            src = top
        return src[i * BLOCK : (i + 1) * BLOCK, j * BLOCK : (j + 1) * BLOCK]

    halves = []
    for pairs, (a, b) in layout(n):
        low = lax.broadcasted_iota(jnp.int32, (BLOCK // 2, BLOCK), 1) < BLOCK // 2
        first, second = block(a, a), block(b, b)
        corner = pltpu.roll(first[BLOCK // 2 :], BLOCK // 2, 1)
        corners = jnp.where(low, corner, second[BLOCK // 2 :])
        halves.append(
            [block(*pair) for pair in pairs]
            + [first[: BLOCK // 2], second[: BLOCK // 2], corners]
        )
    at = 0
    for zero, one in zip(*halves):
        rows = slice(at, at + zero.shape[0])
        keep[rows, :] = jnp.where(core == 0, zero, one)
        send[rows, :] = jnp.where(core == 0, one, zero)
        at += zero.shape[0]


def local_gram(features, core_of, weights=(1, 2)):
    rows, width = features.shape
    n = width // BLOCK
    half = jax.ShapeDtypeStruct((n * (2 * n + 1) * BLOCK // 8, BLOCK), F32)
    plan = cuts(rows, weights)
    return pl.pallas_call(
        functools.partial(gram_kernel, plan, core_of),
        out_shape=(half, half),
        in_specs=[pl.BlockSpec(memory_space=pl.ANY)],
        out_specs=(pl.BlockSpec(memory_space=pltpu.VMEM),) * 2,
        scratch_shapes=[
            pltpu.VMEM((rows, width), BF16),
            pltpu.VMEM((width // 2, width), F32),
            pltpu.VMEM((width // 2, width // 2), F32),
            pltpu.SemaphoreType.DMA((len(plan),)),
        ],
        compiler_params=pltpu.CompilerParams(vmem_limit_bytes=ROOM),
        cost_estimate=pl.CostEstimate(
            flops=2 * rows * width * width, bytes_accessed=2 * rows * width, transcendentals=0
        ),
        name="gram",
    )(pltpu.with_memory_space_constraint(features, pltpu.HBM))


def stacked(a, b):
    ah, am, al = split3(a)
    bh, bm, bl = split3(b)
    left = jnp.concatenate([al, am, ah, am, ah, ah], axis=1)
    right = jnp.concatenate([bh, bm, bl, bh, bm, bh], axis=0)
    return dot(left, right)


def beside_identity(gram, rank):
    lane = lax.broadcasted_iota(jnp.int32, (rank, 2 * rank), 1)
    row = lax.broadcasted_iota(jnp.int32, (rank, 2 * rank), 0)
    return gram + (lane == row).astype(F32)


def gram_of(a, b):
    both = jnp.concatenate([jnp.zeros_like(b), b], axis=0)
    return beside_identity(dot(a, both, NT, HIGHEST), a.shape[0])


def eliminate(tables, outs):
    rank, width = tables[0].shape
    rests = list(tables)

    def spread(rest, skip, at):
        high = rest.shape[0] - skip
        return [
            jnp.broadcast_to(rest[skip:, at + j : at + j + 1], (high, width)) for j in range(8)
        ]

    panels = [spread(rest, 0, rank) for rest in rests]
    for p in range(0, rank, 8):
        last = p + 8 == rank
        look = len(outs) == 1
        ahead = [[] if last or not look else spread(rest, 8, rank + p + 8) for rest in rests]
        for j in range(8):
            for t, out in enumerate(outs):
                columns, rest = panels[t], rests[t]
                column = columns[j]
                pivot = column[j : j + 1, :]
                inverse = 1.0 / pivot
                row = rest[j : j + 1, :]
                out[p + j : p + j + 1, :] = row * lax.rsqrt(pivot)
                for i in range(j + 1, 8):
                    columns[i] = columns[i] - column * (column[i : i + 1, :] * inverse)
                for i in range(len(ahead[t])):
                    factor = column[8 + i : 9 + i, :] * inverse
                    ahead[t][i] = ahead[t][i] - column[8:, :] * factor
                rests[t] = rest - column * (row * inverse)
        rests = [rest[8:, :] for rest in rests]
        if not last:
            panels = ahead if look else [spread(rest, 0, rank + p + 8) for rest in rests]


def eliminate_slowly(gram, table, out):
    rank, width = gram.shape
    table[...] = gram
    lane = lax.broadcasted_iota(jnp.int32, (rank, width), 1)

    def step(k, carry):
        rest = table[...]
        column = jnp.sum(jnp.where(lane == rank + k, rest, 0.0), axis=1, keepdims=True)
        row = table[pl.ds(k, 1), :]
        pivot = jnp.sum(jnp.where(lane[:1] == rank + k, row, 0.0), axis=1, keepdims=True)
        out[pl.ds(k, 1), :] = row * lax.rsqrt(pivot)
        table[...] = rest - column * (row * (1.0 / pivot))
        return carry

    lax.fori_loop(0, rank, step, 0)


def polish(rows):
    rank = rows.shape[0]
    lane = lax.broadcasted_iota(jnp.int32, (rank, rank), 1)
    row = lax.broadcasted_iota(jnp.int32, (rank, rank), 0)
    eye = (lane == row).astype(F32)
    half = jnp.where(lane < row, 1.0, 0.0) + 0.5 * eye
    off = dot(rows, rows, NT, HIGHEST) - eye
    first = off * half
    rough = first.astype(BF16)
    change = (dot(rough, rough) + dot(rough, rough, NT) * half) - first
    high, low = split2(change)
    top, rest = split2(rows)
    return jnp.sum(off * off), rows + ((dot(low, top) + dot(high, rest)) + dot(high, top))


def finish_kernel(
    scale, plan, core_of, mine, other, sketch, features, basis, left, codes,
    parts, table, image_table, hold, weights, held, left_held, codes_held, arrived, gone, done,
):
    rank, width = sketch.shape
    n = width // BLOCK
    fetches = []
    for k, (start, stop) in enumerate(plan):
        rows = pl.ds(start, stop - start)
        copy = pltpu.make_async_copy(features.at[rows], held.at[rows], arrived.at[k])
        copy.start()
        fetches.append(copy)
    core = core_of()

    def store(i, j, block):
        for q, part in enumerate(split3(block)):
            parts[q, i * BLOCK : (i + 1) * BLOCK, j * BLOCK : (j + 1) * BLOCK] = part

    for half, (pairs, diagonal) in enumerate(layout(n)):

        def rows_at(start, size):
            rows = slice(start, start + size)
            return jnp.where(core == half, mine[rows, :], other[rows, :])

        for k, (i, j) in enumerate(pairs):
            block = rows_at(k * BLOCK, BLOCK)
            store(i, j, block)
            store(j, i, block.T)
        at = len(pairs) * BLOCK
        corners = rows_at(at + BLOCK, BLOCK // 2)
        for k, i in enumerate(diagonal):
            corner = corners if k else pltpu.roll(corners, BLOCK // 2, 1)
            block = jnp.concatenate([rows_at(at + k * BLOCK // 2, BLOCK // 2), corner], axis=0)
            lane = lax.broadcasted_iota(jnp.int32, (BLOCK, BLOCK), 1)
            row = lax.broadcasted_iota(jnp.int32, (BLOCK, BLOCK), 0)
            store(i, i, jnp.where((row >= BLOCK // 2) & (lane < BLOCK // 2), block.T, block))

    def times_gram(rows):
        deep = parts.shape[0] * width
        return dot(jnp.concatenate([rows] * 3, axis=1), parts[...].reshape(deep, width))

    def sweep(rows):
        eliminate([gram_of(rows, rows)], [table])
        return stacked(table[:, :rank], rows)

    def scale_left(factor, near):
        for k, part in enumerate(split2(dot(factor, near, NN, HIGHEST) * scale)):
            weights[k * rank : (k + 1) * rank, :] = part

    raw = times_gram(sketch[...])
    wide = sweep(raw)
    distance, polished = polish(wide)
    estimate = polished.astype(BF16)
    near = estimate.astype(F32)
    image = times_gram(estimate)
    eliminate([gram_of(image, near), gram_of(image, image)], [table, image_table])
    scale_left(table[:, :rank], near)
    swept = stacked(image_table[:, :rank], image)
    distance_too, polished = polish(swept)
    hold[...] = polished

    @pl.when(jnp.logical_not(distance + distance_too <= NEAR))
    def _():
        def slow_sweep(rows):
            eliminate_slowly(gram_of(rows, rows), image_table, table)
            return dot(table[:, :rank], rows, NN, HIGHEST)

        estimate = slow_sweep(wide).astype(BF16)
        near = estimate.astype(F32)
        image = times_gram(estimate)
        eliminate_slowly(gram_of(image, near), image_table, table)
        factor = table[:, :rank]
        scale_left(factor, near)
        hold[...] = dot(factor, image, NN, HIGHEST)

        def again(k, carry):
            hold[...] = slow_sweep(hold[...])
            return carry

        lax.fori_loop(0, 2, again, 0)

    own_copy = pltpu.make_async_copy(hold, basis, done)
    own_copy.start()
    weights[2 * rank : 3 * rank, :] = hold[...].astype(BF16)

    sends = [own_copy]
    for k, (start, stop) in enumerate(plan):
        span = pl.ds(start, stop - start)
        own = [
            pltpu.make_async_copy(source.at[:, span], target.at[:, span], gone.at[q, k])
            for q, (source, target) in enumerate(((left_held, left), (codes_held, codes)))
        ]
        sends += own

        def piece(k=k, start=start, stop=stop, own=own):
            fetches[k].wait()
            columns = slice(start, stop)
            out = dot(weights[...], held[start:stop, :], NT)
            left_held[:, columns] = out[rank : 2 * rank] + out[:rank]
            codes_held[:, columns] = out[2 * rank :].astype(BF16)
            for copy in own:
                copy.start()

        pl.when(core >= 0)(piece)
    for copy in sends:
        copy.wait()


def finish(mine, other, sketch_rows, features, scale, core_of, weights=(5, 1)):
    rank, width = sketch_rows.shape
    rows = features.shape[0]
    plan = cuts(rows, weights)
    vmem = pl.BlockSpec(memory_space=pltpu.VMEM)
    hbm = pl.BlockSpec(memory_space=pl.ANY)
    return pl.pallas_call(
        functools.partial(finish_kernel, scale, plan, core_of),
        out_shape=(
            jax.ShapeDtypeStruct((rank, width), F32),
            jax.ShapeDtypeStruct((rank, rows), F32),
            jax.ShapeDtypeStruct((rank, rows), BF16),
        ),
        in_specs=[vmem, vmem, vmem, hbm],
        out_specs=(hbm, hbm, hbm),
        scratch_shapes=[
            pltpu.VMEM((3, width, width), BF16),
            pltpu.VMEM((rank, 2 * rank), F32),
            pltpu.VMEM((rank, 2 * rank), F32),
            pltpu.VMEM((rank, width), F32),
            pltpu.VMEM((3 * rank, width), BF16),
            pltpu.VMEM((rows, width), BF16),
            pltpu.VMEM((rank, rows), F32),
            pltpu.VMEM((rank, rows), BF16),
            pltpu.SemaphoreType.DMA((len(plan),)),
            pltpu.SemaphoreType.DMA((2, len(plan))),
            pltpu.SemaphoreType.DMA(()),
        ],
        compiler_params=pltpu.CompilerParams(vmem_limit_bytes=ROOM),
        name="finish",
    )(mine, other, sketch_rows, pltpu.with_memory_space_constraint(features, pltpu.HBM))


def exchange(parts, axes):
    return lax.all_to_all(parts, axes, split_axis=0, concat_axis=0, tiled=True)


def swap(x):
    return lax.ppermute(x, "c", [(0, 1), (1, 0)])


def sum_everywhere(keep, send):
    slab, line = ("near", "gx"), "far"
    cells, length = lax.axis_size(slab), lax.axis_size(line)
    half = keep + swap(send)
    rows, width = half.shape
    pieces = half.reshape(cells, rows // cells // 2, 2, width)
    share = jnp.sum(exchange(pieces, slab), axis=0)
    share = jnp.sum(exchange(jnp.broadcast_to(share, (length, *share.shape)), line), axis=0)
    mine = exchange(jnp.broadcast_to(share, (cells, *share.shape)), slab).reshape(rows, width)
    return mine, swap(mine)


def core_index():
    return lax.axis_index("c")


def on_device(features, sketch):
    scale = math.sqrt(features.shape[0] * lax.axis_size(("gx", "far", "near", "c")))
    mine, other = sum_everywhere(*local_gram(features, core_index))
    basis, left, codes = finish(mine, other, sketch.T, features, scale, core_index)
    return (basis.T, codes.T, left.T)


def solution(mesh):
    rows, columns = mesh.devices.shape
    mesh = Mesh(mesh.devices.reshape(rows, columns // 4, 2, 2), ("gx", "far", "near", "c"))
    split = P(("gx", "far", "near", "c"), None)
    return jax.shard_map(
        on_device,
        mesh=mesh,
        in_specs=(split, P()),
        out_specs=(P(), split, split),
        check_vma=False,
    )
```

```python
import functools
import math

import jax
import jax.numpy as jnp
from jax import lax
from jax.experimental import pallas as pl
from jax.experimental.pallas import tpu as pltpu
from jax.sharding import Mesh, PartitionSpec as P

BLOCK = 128
ROOM = 24 * 1024 * 1024
HIGHEST = lax.Precision.HIGHEST
NEAR = 1e-5
F32 = jnp.float32
BF16 = jnp.bfloat16
NT = (((1,), (1,)), ((), ()))
NN = (((1,), (0,)), ((), ()))
TN = (((0,), (0,)), ((), ()))


def dot(a, b, dims=NN, precision=None):
    return lax.dot_general(a, b, dims, precision=precision, preferred_element_type=F32)


def split3(x):
    high = x.astype(BF16)
    rest = x - high.astype(F32)
    middle = rest.astype(BF16)
    low = (rest - middle.astype(F32)).astype(BF16)
    return high, middle, low


def split2(x):
    high = x.astype(BF16)
    return high, (x - high.astype(F32)).astype(BF16)


def layout(n):
    pairs = [(i, j) for i in range(n) for j in range(i + 1, n)]
    count = len(pairs) // 2
    return (pairs[:count], (0, 1)), (pairs[count:], (2, 3))


def cuts(rows, weights):
    units = rows // BLOCK
    total = sum(weights)
    edges = [0]
    for k in range(len(weights)):
        edges.append(round(units * sum(weights[: k + 1]) / total) * BLOCK)
    return list(zip(edges[:-1], edges[1:]))


def gram_kernel(plan, core_of, features, keep, send, held, top, bottom, arrived):
    width = features.shape[1]
    n = width // BLOCK
    half = width // 2
    copies = []
    for k, (start, stop) in enumerate(plan):
        rows = pl.ds(start, stop - start)
        copy = pltpu.make_async_copy(features.at[rows], held.at[rows], arrived.at[k])
        copy.start()
        copies.append(copy)
    core = core_of()

    def add(k):
        start, stop = plan[k]
        copies[k].wait()
        f = held[start:stop, :]
        a = dot(f[:, :half], f, TN)
        b = dot(f[:, half:], f[:, half:], TN)
        top[...] = top[...] + a if k else a
        bottom[...] = bottom[...] + b if k else b

    for k in range(len(plan) - 1):
        pl.when(core >= 0)(functools.partial(add, k))
    add(len(plan) - 1)

    def block(i, j):
        if i >= n // 2:
            src, i, j = bottom, i - n // 2, j - n // 2
        else:
            src = top
        return src[i * BLOCK : (i + 1) * BLOCK, j * BLOCK : (j + 1) * BLOCK]

    halves = []
    for pairs, (a, b) in layout(n):
        low = lax.broadcasted_iota(jnp.int32, (BLOCK // 2, BLOCK), 1) < BLOCK // 2
        first, second = block(a, a), block(b, b)
        corner = pltpu.roll(first[BLOCK // 2 :], BLOCK // 2, 1)
        corners = jnp.where(low, corner, second[BLOCK // 2 :])
        halves.append(
            [block(*pair) for pair in pairs]
            + [first[: BLOCK // 2], second[: BLOCK // 2], corners]
        )
    at = 0
    for zero, one in zip(*halves):
        rows = slice(at, at + zero.shape[0])
        keep[rows, :] = jnp.where(core == 0, zero, one)
        send[rows, :] = jnp.where(core == 0, one, zero)
        at += zero.shape[0]


def local_gram(features, core_of, weights=(1, 2)):
    rows, width = features.shape
    n = width // BLOCK
    half = jax.ShapeDtypeStruct((n * (2 * n + 1) * BLOCK // 8, BLOCK), F32)
    plan = cuts(rows, weights)
    return pl.pallas_call(
        functools.partial(gram_kernel, plan, core_of),
        out_shape=(half, half),
        in_specs=[pl.BlockSpec(memory_space=pl.ANY)],
        out_specs=(pl.BlockSpec(memory_space=pltpu.VMEM),) * 2,
        scratch_shapes=[
            pltpu.VMEM((rows, width), BF16),
            pltpu.VMEM((width // 2, width), F32),
            pltpu.VMEM((width // 2, width // 2), F32),
            pltpu.SemaphoreType.DMA((len(plan),)),
        ],
        compiler_params=pltpu.CompilerParams(vmem_limit_bytes=ROOM),
        cost_estimate=pl.CostEstimate(
            flops=2 * rows * width * width, bytes_accessed=2 * rows * width, transcendentals=0
        ),
        name="gram",
    )(pltpu.with_memory_space_constraint(features, pltpu.HBM))


def stacked(a, b):
    ah, am, al = split3(a)
    bh, bm, bl = split3(b)
    left = jnp.concatenate([al, am, ah, am, ah, ah], axis=1)
    right = jnp.concatenate([bh, bm, bl, bh, bm, bh], axis=0)
    return dot(left, right)


def beside_identity(gram, rank):
    lane = lax.broadcasted_iota(jnp.int32, (rank, 2 * rank), 1)
    row = lax.broadcasted_iota(jnp.int32, (rank, 2 * rank), 0)
    return gram + (lane == row).astype(F32)


def gram_of(a, b):
    both = jnp.concatenate([jnp.zeros_like(b), b], axis=0)
    return beside_identity(dot(a, both, NT, HIGHEST), a.shape[0])


def eliminate(tables, outs):
    rank, width = tables[0].shape
    rests = list(tables)

    def spread(rest, skip, at):
        high = rest.shape[0] - skip
        return [
            jnp.broadcast_to(rest[skip:, at + j : at + j + 1], (high, width)) for j in range(8)
        ]

    panels = [spread(rest, 0, rank) for rest in rests]
    for p in range(0, rank, 8):
        last = p + 8 == rank
        look = len(outs) == 1
        ahead = [[] if last or not look else spread(rest, 8, rank + p + 8) for rest in rests]
        for j in range(8):
            for t, out in enumerate(outs):
                columns, rest = panels[t], rests[t]
                column = columns[j]
                pivot = column[j : j + 1, :]
                inverse = 1.0 / pivot
                row = rest[j : j + 1, :]
                out[p + j : p + j + 1, :] = row * lax.rsqrt(pivot)
                for i in range(j + 1, 8):
                    columns[i] = columns[i] - column * (column[i : i + 1, :] * inverse)
                for i in range(len(ahead[t])):
                    factor = column[8 + i : 9 + i, :] * inverse
                    ahead[t][i] = ahead[t][i] - column[8:, :] * factor
                rests[t] = rest - column * (row * inverse)
        rests = [rest[8:, :] for rest in rests]
        if not last:
            panels = ahead if look else [spread(rest, 0, rank + p + 8) for rest in rests]


def eliminate_slowly(gram, table, out):
    rank, width = gram.shape
    table[...] = gram
    lane = lax.broadcasted_iota(jnp.int32, (rank, width), 1)

    def step(k, carry):
        rest = table[...]
        column = jnp.sum(jnp.where(lane == rank + k, rest, 0.0), axis=1, keepdims=True)
        row = table[pl.ds(k, 1), :]
        pivot = jnp.sum(jnp.where(lane[:1] == rank + k, row, 0.0), axis=1, keepdims=True)
        out[pl.ds(k, 1), :] = row * lax.rsqrt(pivot)
        table[...] = rest - column * (row * (1.0 / pivot))
        return carry

    lax.fori_loop(0, rank, step, 0)


def polish(rows):
    rank = rows.shape[0]
    lane = lax.broadcasted_iota(jnp.int32, (rank, rank), 1)
    row = lax.broadcasted_iota(jnp.int32, (rank, rank), 0)
    eye = (lane == row).astype(F32)
    half = jnp.where(lane < row, 1.0, 0.0) + 0.5 * eye
    off = dot(rows, rows, NT, HIGHEST) - eye
    first = off * half
    rough = first.astype(BF16)
    change = (dot(rough, rough) + dot(rough, rough, NT) * half) - first
    high, low = split2(change)
    top, rest = split2(rows)
    return jnp.sum(off * off), rows + ((dot(low, top) + dot(high, rest)) + dot(high, top))


def finish_kernel(
    scale, plan, core_of, mine, other, sketch, features, basis, left, codes,
    parts, table, image_table, hold, weights, held, left_held, codes_held, arrived, gone, done,
):
    rank, width = sketch.shape
    n = width // BLOCK
    fetches = []
    for k, (start, stop) in enumerate(plan):
        rows = pl.ds(start, stop - start)
        copy = pltpu.make_async_copy(features.at[rows], held.at[rows], arrived.at[k])
        copy.start()
        fetches.append(copy)
    core = core_of()

    def store(i, j, block):
        for q, part in enumerate(split3(block)):
            parts[q, i * BLOCK : (i + 1) * BLOCK, j * BLOCK : (j + 1) * BLOCK] = part

    for half, (pairs, diagonal) in enumerate(layout(n)):

        def rows_at(start, size):
            rows = slice(start, start + size)
            return jnp.where(core == half, mine[rows, :], other[rows, :])

        for k, (i, j) in enumerate(pairs):
            block = rows_at(k * BLOCK, BLOCK)
            store(i, j, block)
            store(j, i, block.T)
        at = len(pairs) * BLOCK
        corners = rows_at(at + BLOCK, BLOCK // 2)
        for k, i in enumerate(diagonal):
            corner = corners if k else pltpu.roll(corners, BLOCK // 2, 1)
            block = jnp.concatenate([rows_at(at + k * BLOCK // 2, BLOCK // 2), corner], axis=0)
            lane = lax.broadcasted_iota(jnp.int32, (BLOCK, BLOCK), 1)
            row = lax.broadcasted_iota(jnp.int32, (BLOCK, BLOCK), 0)
            store(i, i, jnp.where((row >= BLOCK // 2) & (lane < BLOCK // 2), block.T, block))

    def times_gram(rows):
        deep = parts.shape[0] * width
        return dot(jnp.concatenate([rows] * 3, axis=1), parts[...].reshape(deep, width))

    def sweep(rows):
        eliminate([gram_of(rows, rows)], [table])
        return stacked(table[:, :rank], rows)

    def scale_left(factor, near):
        for k, part in enumerate(split2(dot(factor, near, NN, HIGHEST) * scale)):
            weights[k * rank : (k + 1) * rank, :] = part

    raw = times_gram(sketch[...])
    wide = sweep(raw)
    distance, polished = polish(wide)
    estimate = polished.astype(BF16)
    near = estimate.astype(F32)
    image = times_gram(estimate)
    eliminate([gram_of(image, near), gram_of(image, image)], [table, image_table])
    scale_left(table[:, :rank], near)
    swept = stacked(image_table[:, :rank], image)
    distance_too, polished = polish(swept)
    hold[...] = polished

    @pl.when(jnp.logical_not(distance + distance_too <= NEAR))
    def _():
        def slow_sweep(rows):
            eliminate_slowly(gram_of(rows, rows), image_table, table)
            return dot(table[:, :rank], rows, NN, HIGHEST)

        estimate = slow_sweep(wide).astype(BF16)
        near = estimate.astype(F32)
        image = times_gram(estimate)
        eliminate_slowly(gram_of(image, near), image_table, table)
        factor = table[:, :rank]
        scale_left(factor, near)
        hold[...] = dot(factor, image, NN, HIGHEST)

        def again(k, carry):
            hold[...] = slow_sweep(hold[...])
            return carry

        lax.fori_loop(0, 2, again, 0)

    own_copy = pltpu.make_async_copy(hold, basis, done)
    own_copy.start()
    weights[2 * rank : 3 * rank, :] = hold[...].astype(BF16)

    sends = [own_copy]
    for k, (start, stop) in enumerate(plan):
        span = pl.ds(start, stop - start)
        own = [
            pltpu.make_async_copy(source.at[:, span], target.at[:, span], gone.at[q, k])
            for q, (source, target) in enumerate(((left_held, left), (codes_held, codes)))
        ]
        sends += own

        def piece(k=k, start=start, stop=stop, own=own):
            fetches[k].wait()
            columns = slice(start, stop)
            out = dot(weights[...], held[start:stop, :], NT)
            left_held[:, columns] = out[rank : 2 * rank] + out[:rank]
            codes_held[:, columns] = out[2 * rank :].astype(BF16)
            for copy in own:
                copy.start()

        pl.when(core >= 0)(piece)
    for copy in sends:
        copy.wait()


def finish(mine, other, sketch_rows, features, scale, core_of, weights=(5, 1)):
    rank, width = sketch_rows.shape
    rows = features.shape[0]
    plan = cuts(rows, weights)
    vmem = pl.BlockSpec(memory_space=pltpu.VMEM)
    hbm = pl.BlockSpec(memory_space=pl.ANY)
    return pl.pallas_call(
        functools.partial(finish_kernel, scale, plan, core_of),
        out_shape=(
            jax.ShapeDtypeStruct((rank, width), F32),
            jax.ShapeDtypeStruct((rank, rows), F32),
            jax.ShapeDtypeStruct((rank, rows), BF16),
        ),
        in_specs=[vmem, vmem, vmem, hbm],
        out_specs=(hbm, hbm, hbm),
        scratch_shapes=[
            pltpu.VMEM((3, width, width), BF16),
            pltpu.VMEM((rank, 2 * rank), F32),
            pltpu.VMEM((rank, 2 * rank), F32),
            pltpu.VMEM((rank, width), F32),
            pltpu.VMEM((3 * rank, width), BF16),
            pltpu.VMEM((rows, width), BF16),
            pltpu.VMEM((rank, rows), F32),
            pltpu.VMEM((rank, rows), BF16),
            pltpu.SemaphoreType.DMA((len(plan),)),
            pltpu.SemaphoreType.DMA((2, len(plan))),
            pltpu.SemaphoreType.DMA(()),
        ],
        compiler_params=pltpu.CompilerParams(vmem_limit_bytes=ROOM),
        name="finish",
    )(mine, other, sketch_rows, pltpu.with_memory_space_constraint(features, pltpu.HBM))


def exchange(parts, axes):
    return lax.all_to_all(parts, axes, split_axis=0, concat_axis=0, tiled=True)


def swap(x):
    return lax.ppermute(x, "c", [(0, 1), (1, 0)])


def sum_everywhere(keep, send):
    slab, line = ("near", "gx"), ("low", "high")
    cells, length = lax.axis_size(slab), lax.axis_size(line)
    half = keep + swap(send)
    rows, width = half.shape
    pieces = half.reshape(cells, rows // cells // 2, 2, width)
    share = jnp.sum(exchange(pieces, slab), axis=0)
    share = jnp.sum(exchange(jnp.broadcast_to(share, (length, *share.shape)), line), axis=0)
    mine = exchange(jnp.broadcast_to(share, (cells, *share.shape)), slab).reshape(rows, width)
    return mine, swap(mine)


def core_index():
    return lax.axis_index("c")


def on_device(features, sketch):
    scale = math.sqrt(features.shape[0] * lax.axis_size(("gx", "high", "low", "near", "c")))
    mine, other = sum_everywhere(*local_gram(features, core_index))
    basis, left, codes = finish(mine, other, sketch.T, features, scale, core_index)
    return (basis.T, codes.T, left.T)


def solution(mesh):
    rows, columns = mesh.devices.shape
    mesh = Mesh(mesh.devices.reshape(rows, columns // 8, 2, 2, 2), ("gx", "high", "low", "near", "c"))
    split = P(("gx", "high", "low", "near", "c"), None)
    return jax.shard_map(
        on_device,
        mesh=mesh,
        in_specs=(split, P()),
        out_specs=(P(), split, split),
        check_vma=False,
    )
```
